256 devices in a mesh: pipe: 4 (over y), expert: 64 (over x, z, core).
Axes of the slice: x: 4, y: 4, z: 8, core: 2. Of those that a mesh axis runs over, the one named last changes fastest.
Arguments:
- inputs: bfloat16 [4, 8192, 7168], P('pipe', 'expert'), may hold values from -6 to 6
- out_grads: bfloat16 [4, 8192, 7168], P('pipe', 'expert'), may hold values from -6 to 6
- routes: int32 [4, 8192, 8], P('pipe', 'expert'), may hold values from 0 to 255, as said below
- gates: float32 [4, 8192, 8], P('pipe', 'expert'), may hold values from 0.1 to 1
- norm_gain: float32 [4, 7168], P('pipe'), may hold values from 0.5 to 1.5
- w_gate: bfloat16 [4, 7168, 8192], P('pipe', None, 'expert'), may hold values from -0.0625 to 0.0625
- w_up: bfloat16 [4, 7168, 8192], P('pipe', None, 'expert'), may hold values from -0.0625 to 0.0625
- w_down: bfloat16 [4, 8192, 7168], P('pipe', 'expert'), may hold values from -0.125 to 0.125
Outputs:
- next_inputs: bfloat16 [4, 8192, 7168], P('pipe', 'expert')
- prior_grads: bfloat16 [4, 8192, 7168], P('pipe', 'expert')
The draws below stay inside these ranges and needn't reach their ends.
Inputs may be any that keep to these rules, and one draw needn't show every extreme that they name: `routes`: of the 128 tokens of one device, at most 6 name any one expert id below 4; in every section some id below 4 is named by exactly 6 tokens of every device, and some device has exactly 6 tokens naming each id below 4. A token names each id below 4 at most once.
All inputs are finite; a program needn't handle non-finite values.
Results may differ from the reference program's by a relative error of at most 0.0045.
Values may be sent and summed in bfloat16 or wider, within the bound.
No kernel may reach another device: no remote copies, remote signals or barrier semaphores. Data moves between devices by JAX's collectives and lax.ppermute only.
A program may use at most 128 MiB of HBM per device.

```python
import math
import jax
import jax.numpy as jnp
from jax import lax

D = 7168
FF = 2048
NE = 256
TOPK = 8
EXP_WIN = 4
CAP = 6
TOK_DEV = 128
SECTIONS = 4
BLOCKS = 64
SPLIT = 16
HS = 128
TOKENS = 8192


def draw_routes(key, part):
    key_hot, key_count, key_rank, key_perm, key_other, key_full = jax.random.split(key, 6)
    hottest = jax.random.randint(key_hot, (SECTIONS, 1, 1), 0, EXP_WIN)
    counts = jax.random.randint(key_count, (SECTIONS, BLOCKS, EXP_WIN), 0, CAP + 1)
    counts = jnp.where(jnp.arange(EXP_WIN)[None, None, :] == hottest, CAP, counts)
    full_block = jax.random.randint(key_full, (SECTIONS, 1, 1), 0, BLOCKS)
    counts = jnp.where(jnp.arange(BLOCKS)[None, :, None] == full_block, CAP, counts)
    scores = jax.random.randint(key_rank, (SECTIONS, BLOCKS, EXP_WIN, TOK_DEV), 0, 1 << 20) * TOK_DEV + jnp.arange(TOK_DEV, dtype=jnp.int32)
    order = jnp.argsort(scores, axis=-1)
    ranking = jnp.argsort(order, axis=-1)
    picked = ranking < counts[..., None]
    picked = jnp.transpose(picked, (0, 1, 3, 2)).reshape(SECTIONS, TOKENS, EXP_WIN)
    window = jnp.pad(picked, ((0, 0), (0, 0), (0, TOPK - EXP_WIN)))
    others = jax.random.randint(key_other, (SECTIONS, TOKENS, TOPK), EXP_WIN, NE)
    virtual = jnp.arange(TOPK, dtype=jnp.int32)
    values = jnp.where(window, virtual[None, None, :], others)
    perm_scores = jax.random.randint(key_perm, (SECTIONS, TOKENS, TOPK), 0, 1 << 20) * TOPK + virtual
    shuffle = jnp.argsort(perm_scores, axis=-1)
    return jnp.take_along_axis(values, shuffle, axis=-1).astype(jnp.int32)


def level_of(key, dims, pieces, least, top_value):
    loudness, own = 1.0, jax.random.fold_in(key, 6)
    for dim, parts in pieces:
        heights = jnp.exp(jax.random.uniform(jax.random.fold_in(own, dim), (parts,), jnp.float32, least / len(pieces), top_value / len(pieces)))
        loudness = loudness * jnp.repeat(heights, dims[dim] // parts).reshape([-1 if axis == dim else 1 for axis in range(len(dims))])
    return loudness


def normal_values(key, extent, scale, bound, pieces=(), held_as=jnp.bfloat16):
    values = scale * jax.random.normal(key, extent, jnp.float32)
    if pieces:
        values = values * level_of(key, extent, pieces, -0.22, 0.18)
    return jnp.clip(values, -bound, bound).astype(held_as)


def setup_inputs(seed: int = 0) -> dict:
    seeds = jax.random.split(jax.random.key(seed), 9)
    inputs = normal_values(seeds[0], (SECTIONS, TOKENS, D), 1.0, 6.0, ((0, 4), (1, 64)))
    out_grads = normal_values(seeds[1], (SECTIONS, TOKENS, D), 1.0, 6.0, ((0, 4), (1, 64)))
    routes = draw_routes(jax.random.fold_in(seeds[8], 71), 0)
    gates = jnp.clip(jnp.exp(math.log(1.0) - 2.3025851 * jax.random.uniform(seeds[3], (SECTIONS, TOKENS, TOPK), jnp.float32) ** level_of(seeds[3], (SECTIONS, TOKENS, TOPK), ((0, 4), (1, 64)), -0.2, 0.2)), 0.1, 1.0)
    norm_gain = jnp.clip(1.0 + 0.1 * jax.random.normal(seeds[4], (SECTIONS, D), jnp.float32), 0.5, 1.5)
    w_gate = normal_values(seeds[5], (SECTIONS, D, EXP_WIN * FF), D ** -0.5, 0.0625, ((0, 4), (2, 64)))
    w_up = normal_values(seeds[6], (SECTIONS, D, EXP_WIN * FF), D ** -0.5, 0.0625, ((0, 4), (2, 64)))
    w_down = normal_values(seeds[7], (SECTIONS, EXP_WIN * FF, D), FF ** -0.5, 0.125, ((0, 4), (1, 64)))
    return {"inputs": inputs, "out_grads": out_grads, "routes": routes, "gates": gates, "norm_gain": norm_gain, "w_gate": w_gate, "w_up": w_up, "w_down": w_down}


EPSILON = 1e-06

def one_section(held, incoming, route_ids, gate_vals, gain, gate_w, up_w, down_w):
    held_float = held.astype(jnp.float32)
    scale = lax.rsqrt(lax.optimization_barrier(jnp.mean(held_float * held_float, axis=1, keepdims=True)) + EPSILON)
    normed = (held_float * scale * gain[None, :]).astype(jnp.bfloat16)
    experts = jnp.arange(EXP_WIN, dtype=jnp.int32)
    named = route_ids[:, :, None] == experts[None, None, :]
    routed = jnp.any(named, axis=1)
    weight_of = lax.optimization_barrier(jnp.sum(jnp.where(named, gate_vals[:, :, None], jnp.float32(0.0)), axis=1))
    routed_int = routed.astype(jnp.int32)
    blocked = routed_int.reshape(BLOCKS, TOK_DEV, EXP_WIN)
    position = (jnp.cumsum(blocked, axis=1) - blocked).reshape(TOKENS, EXP_WIN)
    block_of = jnp.arange(TOKENS, dtype=jnp.int32) // TOK_DEV
    token_ids = jnp.arange(TOKENS, dtype=jnp.int32)
    combined = jnp.zeros((TOKENS, D), jnp.float32)
    normed_grad = jnp.zeros((TOKENS, D), jnp.float32)
    slot_count = BLOCKS * CAP
    for expert in range(EXP_WIN):
        target = jnp.where(routed[:, expert], block_of * CAP + position[:, expert], slot_count).astype(jnp.int32)
        token_of = jnp.zeros((slot_count,), jnp.int32).at[target].set(token_ids, mode='drop')
        live = jnp.zeros((slot_count,), jnp.bool_).at[target].set(True, mode='drop')
        rows = jnp.where(live[:, None], normed[token_of], jnp.zeros((), jnp.bfloat16))
        weight_rows = jnp.where(live, weight_of[token_of, expert], jnp.float32(0.0))
        grad_rows = (weight_rows[:, None] * incoming[token_of].astype(jnp.float32)).astype(jnp.bfloat16)
        gate_cols = gate_w[:, expert * FF:(expert + 1) * FF]
        up_cols = up_w[:, expert * FF:(expert + 1) * FF]
        down_rows = down_w[expert * FF:(expert + 1) * FF, :]
        gate_pre = jnp.dot(rows, gate_cols, preferred_element_type=jnp.float32)
        up_pre = jnp.dot(rows, up_cols, preferred_element_type=jnp.float32)
        sigma = jax.nn.sigmoid(gate_pre)
        silu = gate_pre * sigma
        hidden = (silu * up_pre).astype(jnp.bfloat16)
        hidden_grad = jnp.dot(grad_rows, down_rows.T, preferred_element_type=jnp.float32)
        gate_grad = (hidden_grad * up_pre * sigma * (1.0 + gate_pre * (1.0 - sigma))).astype(jnp.bfloat16)
        up_grad = (hidden_grad * silu).astype(jnp.bfloat16)
        out_rows = jnp.zeros((slot_count, D), jnp.float32)
        in_rows = jnp.zeros((slot_count, D), jnp.float32)
        for group in range(SPLIT):
            low = group * HS
            high = low + HS
            part = jnp.dot(hidden[:, low:high], down_rows[low:high, :], preferred_element_type=jnp.float32)
            out_rows = out_rows + part.astype(jnp.bfloat16).astype(jnp.float32)
            back = jnp.dot(gate_grad[:, low:high], gate_cols[:, low:high].T, preferred_element_type=jnp.float32)
            back = back + jnp.dot(up_grad[:, low:high], up_cols[:, low:high].T, preferred_element_type=jnp.float32)
            in_rows = in_rows + back.astype(jnp.bfloat16).astype(jnp.float32)
        combined = combined.at[token_of].add(jnp.where(live[:, None], weight_rows[:, None] * out_rows, jnp.float32(0.0)))
        normed_grad = normed_grad.at[token_of].add(jnp.where(live[:, None], in_rows, jnp.float32(0.0)))
    layer_out = (held_float + combined).astype(jnp.bfloat16)
    through = lax.optimization_barrier(jnp.sum(held_float * gain[None, :] * normed_grad, axis=1, keepdims=True))
    input_grad = incoming.astype(jnp.float32) + scale * gain[None, :] * normed_grad - held_float * (scale * scale * scale) / D * through
    return (layer_out, input_grad.astype(jnp.bfloat16))

def reference(inputs, out_grads, routes, gates, norm_gain, w_gate, w_up, w_down):
    outs_list = []
    grads_list = []
    for section in range(SECTIONS):
        layer_out, input_grad = one_section(inputs[section], out_grads[section], routes[section], gates[section], norm_gain[section], w_gate[section], w_up[section], w_down[section])
        outs_list.append(layer_out)
        grads_list.append(input_grad)
    layer_outs = jnp.stack(outs_list)
    input_grads = jnp.stack(grads_list)
    return (jnp.roll(layer_outs, 1, axis=0), jnp.roll(input_grads, -1, axis=0))
```

```python
import jax
import jax.numpy as jnp
from jax import lax
from jax.sharding import PartitionSpec as P

EXP_WIN = 4
CAP = 6
EPSILON = 1e-06
NX, NZ, NC = 4, 8, 2
BOTH = ("pipe", "expert")


def move(block, dy=0, dx=0, dz=0, dc=0):
    ny = lax.axis_size("pipe")
    route = []
    for y in range(ny):
        for x in range(NX):
            for z in range(NZ):
                for c in range(NC):
                    a = ((y * NX + x) * NZ + z) * NC + c
                    b = (((y + dy) % ny * NX + (x + dx) % NX) * NZ + (z + dz) % NZ) * NC + (c + dc) % NC
                    route.append((a, b))
    return lax.ppermute(block, BOTH, route)


def to_experts(rows):
    blocks = [rows[k * CAP : (k + 1) * CAP] for k in range(NX)]
    return jnp.concatenate([blocks[0]] + [move(blocks[k], dx=k) for k in range(1, NX)], axis=0)


def from_experts(rows, dy):
    blocks = [rows[k * CAP : (k + 1) * CAP] for k in range(NX)]
    return jnp.concatenate([move(blocks[k], dx=-k, dy=dy) for k in range(NX)], axis=0)


def gather_z(chunk, up):
    got = {0: chunk}
    below = above = chunk
    for step in range(1, 5):
        if step < 4 or up:
            below = move(below, dz=1)
            got[step] = below
        if step < 4 or not up:
            above = move(above, dz=-1)
            got[NZ - step] = above
    return [got[j] for j in range(NZ)]


def reduce_z(parts, up):
    def chain(order, dz):
        held = parts[order[0]].astype(jnp.bfloat16)
        for j in order[1:]:
            held = (move(held, dz=dz).astype(jnp.float32) + parts[j]).astype(jnp.bfloat16)
        return move(held, dz=dz).astype(jnp.float32)

    above = [5, 6, 7]
    below = [3, 2, 1]
    if up:
        above = [4] + above
    else:
        below = [4] + below
    return parts[0] + chain(above, 1) + chain(below, -1)


def on_device(inputs, out_grads, routes, gates, norm_gain, w_gate, w_up, w_down):
    held = inputs[0]
    incoming = out_grads[0]
    width = held.shape[1]
    tokens = held.shape[0]
    f32, bf16 = jnp.float32, jnp.bfloat16

    held_next = move(held, dy=1)
    incoming_next = move(incoming, dy=-1)
    gain = norm_gain
    gain_next = move(gain, dy=-1)

    gate_w = jnp.concatenate([w_gate[0], move(w_gate[0], dc=1)], axis=1)
    up_w = jnp.concatenate([w_up[0], move(w_up[0], dc=1)], axis=1)
    down_w = jnp.concatenate([w_down[0], move(w_down[0], dc=1)], axis=0)

    column = lax.axis_index("expert") // (NZ * NC)
    experts = (column + jnp.arange(EXP_WIN, dtype=jnp.int32)) % EXP_WIN
    named = routes[0][:, :, None] == experts[None, None, :]
    routed = jnp.any(named, axis=1)
    weight_of = jnp.sum(jnp.where(named, gates[0][:, :, None], f32(0.0)), axis=1)
    token = jnp.arange(tokens, dtype=jnp.int32)
    earlier = (token[None, :] < token[:, None]).astype(bf16)
    position = jnp.dot(earlier, routed.astype(bf16), preferred_element_type=f32)
    slot_ids = jnp.arange(CAP, dtype=jnp.int32).astype(f32)
    chosen = routed.T[:, None, :] & (position.T[:, None, :] == slot_ids[None, :, None])
    slot_weights = jnp.where(chosen, weight_of.T[:, None, :], f32(0.0)).reshape(-1, tokens)
    chosen = chosen.reshape(-1, tokens)
    pick = chosen.astype(bf16)
    weight = jnp.sum(slot_weights, axis=1, keepdims=True)
    picked = jnp.dot(pick, held, preferred_element_type=f32)
    scale = lax.rsqrt(jnp.mean(picked * picked, axis=1, keepdims=True) + EPSILON)
    rows = (picked * scale * gain).astype(bf16)
    grads = (weight * jnp.dot(pick, incoming, preferred_element_type=f32)).astype(bf16)

    weights_next = move(slot_weights, dy=1)
    scales_next = move(jnp.where(chosen, scale, f32(0.0)), dy=-1)
    picked_next = move(picked.astype(bf16), dy=-1)

    all_rows = jnp.concatenate(gather_z(to_experts(rows), True), axis=0)
    all_grads = jnp.concatenate(gather_z(to_experts(grads), False), axis=0)

    gate_pre = jnp.dot(all_rows, gate_w, preferred_element_type=f32)
    up_pre = jnp.dot(all_rows, up_w, preferred_element_type=f32)
    sigma = jax.nn.sigmoid(gate_pre)
    silu = gate_pre * sigma
    hidden = (silu * up_pre).astype(bf16)
    out_part = jnp.dot(hidden, down_w, preferred_element_type=f32)
    out_part = out_part.reshape(NZ, -1, width)
    contract = (((1,), (1,)), ((), ()))
    hidden_grad = lax.dot_general(all_grads, down_w, contract, preferred_element_type=f32)
    gate_grad = (hidden_grad * up_pre * sigma * (1.0 + gate_pre * (1.0 - sigma))).astype(bf16)
    up_grad = (hidden_grad * silu).astype(bf16)
    in_part = lax.dot_general(gate_grad, gate_w, contract, preferred_element_type=f32)
    in_part = in_part + lax.dot_general(up_grad, up_w, contract, preferred_element_type=f32)
    in_part = in_part.reshape(NZ, -1, width)

    out_sum = reduce_z([out_part[j] for j in range(NZ)], True).astype(bf16)
    in_sum = reduce_z([in_part[j] for j in range(NZ)], False).astype(bf16)
    out_slots = from_experts(out_sum, 1).astype(f32)
    in_slots = from_experts(in_sum, -1).astype(f32)

    lead = (((0,), (0,)), ((), ()))
    combined = lax.dot_general(
        weights_next, out_slots, lead, precision=lax.Precision.HIGHEST, preferred_element_type=f32
    )
    next_inputs = (held_next.astype(f32) + combined).astype(bf16)

    scale_next = jnp.sum(scales_next, axis=1, keepdims=True)
    from_x = picked_next.astype(f32)
    through = jnp.sum(from_x * gain_next * in_slots, axis=1, keepdims=True)
    change = scale_next * gain_next * in_slots - from_x * (scale_next * scale_next * scale_next) / width * through
    spread = lax.dot_general(
        (scales_next > 0).astype(f32), change, lead, precision=lax.Precision.HIGHEST, preferred_element_type=f32
    )
    prior_grads = (incoming_next.astype(f32) + spread).astype(bf16)
    return (next_inputs[None], prior_grads[None])


def solution(mesh):
    return jax.shard_map(
        on_device,
        mesh=mesh,
        in_specs=(
            P("pipe", "expert", None),
            P("pipe", "expert", None),
            P("pipe", "expert", None),
            P("pipe", "expert", None),
            P("pipe", None),
            P("pipe", None, "expert"),
            P("pipe", None, "expert"),
            P("pipe", "expert", None),
        ),
        out_specs=(P("pipe", "expert", None), P("pipe", "expert", None)),
        check_vma=False,
    )
```

```python
import jax
import jax.numpy as jnp
from jax import lax
from jax.experimental import pallas as pl
from jax.experimental.pallas import tpu as pltpu
from jax.sharding import PartitionSpec as P

EXP_WIN = 4
CAP = 6
EPSILON = 1e-06
NX, NZ, NC = 4, 8, 2
BOTH = ("pipe", "expert")
STRIPS = 7
LAST = (((1,), (1,)), ((), ()))


def move(block, dy=0, dx=0, dz=0, dc=0):
    ny = lax.axis_size("pipe")
    route = []
    for y in range(ny):
        for x in range(NX):
            for z in range(NZ):
                for c in range(NC):
                    a = ((y * NX + x) * NZ + z) * NC + c
                    b = (((y + dy) % ny * NX + (x + dx) % NX) * NZ + (z + dz) % NZ) * NC + (c + dc) % NC
                    route.append((a, b))
    return lax.ppermute(block, BOTH, route)


def to_experts(rows):
    blocks = [rows[k * CAP : (k + 1) * CAP] for k in range(NX)]
    got = jnp.concatenate([blocks[0]] + [move(blocks[k], dx=k) for k in range(1, NX)], axis=0)
    return lax.optimization_barrier(got)


def from_experts(rows, dy):
    blocks = [rows[k * CAP : (k + 1) * CAP] for k in range(NX)]
    return jnp.concatenate([move(blocks[k], dx=-k, dy=dy) for k in range(NX)], axis=0)


def after(values, *needed):
    return lax.optimization_barrier((values, needed))[0]


def add(part, got):
    return (got.astype(jnp.float32) + part).astype(jnp.bfloat16)


def product(a, b):
    return jnp.dot(a, b, preferred_element_type=jnp.float32)


def product_t(a, b):
    return lax.dot_general(a, b, LAST, preferred_element_type=jnp.float32)


def experts_kernel(count, forward, backward, *refs):
    refs = list(refs)
    take = lambda n: [refs.pop(0) for _ in range(n)]
    rows = take(count) if forward else []
    grads = take(count) if backward else []
    pre_in = take(0 if forward else 2)
    sources = take(6)
    outs = take(count) if forward else []
    ins = take(count) if backward else []
    pre_out = take(0 if backward else 2)
    gate_w, up_w, down_w, sems = refs
    width = down_w.shape[1]
    each = sources[4].shape[0]
    strip = width // STRIPS
    high = rows[0].shape[0] if forward else grads[0].shape[0]

    def copies(s):
        at = pl.ds(s * strip, strip)
        pairs = []
        if forward or backward:
            for core in range(NC):
                lanes = pl.ds(core * each, each)
                pairs.append((sources[core].at[at, :], gate_w.at[at, lanes]))
                pairs.append((sources[2 + core].at[at, :], up_w.at[at, lanes]))
                pairs.append((sources[4 + core].at[:, at], down_w.at[lanes, at]))
        return [pltpu.make_async_copy(a, b, sems.at[s, i]) for i, (a, b) in enumerate(pairs)]

    for s in range(STRIPS):
        for copy in copies(s):
            copy.start()

    def stack(blocks, at):
        if len(blocks) == 1:
            return blocks[0][:, at]
        return jnp.concatenate([b[:, at].astype(jnp.float32) for b in blocks], axis=0).astype(jnp.bfloat16)

    shape = (count * high, NC * each)
    gate_pre = up_pre = hidden_grad = jnp.zeros(shape, jnp.float32)
    if not forward:
        gate_pre, up_pre = pre_in[0][...], pre_in[1][...]
    for s in range(STRIPS):
        for copy in copies(s):
            copy.wait()
        at = slice(s * strip, (s + 1) * strip)
        if forward:
            here = stack(rows, at)
            gate_pre += product(here, gate_w[at, :])
            up_pre += product(here, up_w[at, :])
        if backward:
            hidden_grad += product_t(stack(grads, at), down_w[:, at])
    sigma = jax.nn.sigmoid(gate_pre)
    silu = gate_pre * sigma
    if not backward:
        pre_out[0][...] = gate_pre
        pre_out[1][...] = up_pre
    if forward:
        hidden = (silu * up_pre).astype(jnp.bfloat16)
    if backward:
        gate_grad = (hidden_grad * up_pre * sigma * (1.0 + gate_pre * (1.0 - sigma))).astype(jnp.bfloat16)
        up_grad = (hidden_grad * silu).astype(jnp.bfloat16)
    for s in range(STRIPS):
        at = slice(s * strip, (s + 1) * strip)
        if forward:
            got = product(hidden, down_w[:, at])
            for i in range(count):
                outs[i][:, at] = got[i * high : (i + 1) * high]
        if backward:
            got = product_t(gate_grad, gate_w[at, :]) + product_t(up_grad, up_w[at, :])
            for i in range(count):
                ins[i][:, at] = got[i * high : (i + 1) * high]


def experts(rows, grads, weights, pre=None):
    forward, backward = bool(rows), bool(grads)
    count = max(len(rows), len(grads))
    high, width = (rows or grads)[0].shape
    units = NC * weights[0].shape[1]
    part = jax.ShapeDtypeStruct((high, width), jnp.float32)
    shapes = [part] * (len(rows) + len(grads))
    if not backward:
        shapes += [jax.ShapeDtypeStruct((count * high, units), jnp.float32)] * 2
    vmem = pl.BlockSpec(memory_space=pltpu.VMEM)
    given = [*rows, *grads] + ([] if forward else list(pre))
    passes = 3 * (forward + backward)
    got = pl.pallas_call(
        lambda *refs: experts_kernel(count, forward, backward, *refs),
        out_shape=shapes,
        in_specs=[vmem] * len(given) + [pl.BlockSpec(memory_space=pl.ANY)] * 6,
        out_specs=[vmem] * len(shapes),
        scratch_shapes=[
            pltpu.VMEM((width, units), jnp.bfloat16),
            pltpu.VMEM((width, units), jnp.bfloat16),
            pltpu.VMEM((units, width), jnp.bfloat16),
            pltpu.SemaphoreType.DMA((STRIPS, 6)),
        ],
        compiler_params=pltpu.CompilerParams(vmem_limit_bytes=28 * 2**20),
        cost_estimate=pl.CostEstimate(
            flops=2 * passes * count * high * width * units, bytes_accessed=6 * width * units, transcendentals=0
        ),
    )(*given, *weights)
    return got


def on_device(inputs, out_grads, routes, gates, norm_gain, w_gate, w_up, w_down):
    held = inputs[0]
    incoming = out_grads[0]
    width = held.shape[1]
    tokens = held.shape[0]
    f32, bf16 = jnp.float32, jnp.bfloat16

    gain = norm_gain
    gain_next = move(gain, dy=-1)

    swapped = [move(w[0], dc=1) for w in (w_gate, w_up, w_down)]

    column = lax.axis_index("expert") // (NZ * NC)
    here = (column + jnp.arange(EXP_WIN, dtype=jnp.int32)) % EXP_WIN
    named = routes[0][:, :, None] == here[None, None, :]
    routed = jnp.any(named, axis=1)
    weight_of = jnp.sum(jnp.where(named, gates[0][:, :, None], f32(0.0)), axis=1)
    token = jnp.arange(tokens, dtype=jnp.int32)
    earlier = (token[None, :] < token[:, None]).astype(bf16)
    position = jnp.dot(earlier, routed.astype(bf16), preferred_element_type=f32)
    slot_ids = jnp.arange(CAP, dtype=jnp.int32).astype(f32)
    chosen = routed.T[:, None, :] & (position.T[:, None, :] == slot_ids[None, :, None])
    slot_weights = jnp.where(chosen, weight_of.T[:, None, :], f32(0.0)).reshape(-1, tokens)
    chosen = chosen.reshape(-1, tokens)
    pick = chosen.astype(bf16)
    weight = jnp.sum(slot_weights, axis=1, keepdims=True)
    picked = jnp.dot(pick, held, preferred_element_type=f32)
    scale = lax.rsqrt(jnp.mean(picked * picked, axis=1, keepdims=True) + EPSILON)
    rows = (picked * scale * gain).astype(bf16)
    grads = (weight * jnp.dot(pick, incoming, preferred_element_type=f32)).astype(bf16)

    weights_next = move(slot_weights, dy=1)
    scales_next = move(jnp.where(chosen, scale, f32(0.0)), dy=-1)
    picked_next = move(picked.astype(bf16), dy=-1)

    small = (gain_next, weights_next, scales_next, picked_next)
    (held_sent, incoming_sent), small = lax.optimization_barrier(((held, incoming), small))
    held_next = move(held_sent, dy=1)
    incoming_next = move(incoming_sent, dy=-1)

    rows = {0: to_experts(rows)}
    grads = {0: to_experts(grads)}
    rows[1], rows[7] = move(rows[0], dz=1), move(rows[0], dz=-1)
    grads[1], grads[7] = move(grads[0], dz=1), move(grads[0], dz=-1)

    rows[1], rows[7], swapped = after((rows[1], rows[7], swapped))
    weights = [w_gate[0], swapped[0], w_up[0], swapped[1], w_down[0], swapped[2]]
    rows[2], rows[6] = move(rows[1], dz=1), move(rows[7], dz=-1)
    grads[1], grads[7] = after((grads[1], grads[7]))
    grads[2], grads[6] = move(grads[1], dz=1), move(grads[7], dz=-1)

    out_part, in_part = {}, {}

    def work(group):
        got = experts([rows[j] for j in group], [grads[j] for j in group], weights)
        for i, j in enumerate(group):
            out_part[j], in_part[j] = got[i], got[len(group) + i]

    work((0, 1, 7))
    rows[2], rows[6] = after((rows[2], rows[6]), out_part[0])
    rows[3], rows[5] = move(rows[2], dz=1), move(rows[6], dz=-1)
    grads[2], grads[6] = after((grads[2], grads[6]))
    grads[3], grads[5] = move(grads[2], dz=1), move(grads[6], dz=-1)

    work((2, 6))
    rows[3], rows[5] = after((rows[3], rows[5]), out_part[2])
    rows[4] = move(rows[3], dz=1)
    grads[3], grads[5] = after((grads[3], grads[5]))
    grads[4] = move(grads[5], dz=-1)

    work((3, 5))
    half = jnp.bfloat16
    out_up = move(out_part[5].astype(half), dz=1)
    in_down = move(in_part[3].astype(half), dz=-1)
    rows[4] = after(rows[4], out_part[3])
    out_part[4], *pre = experts([rows[4]], [], weights)
    out_down = move(out_part[4].astype(half), dz=-1)
    grads[4] = after(grads[4], out_part[4])
    (in_part[4],) = experts([], [grads[4]], weights, pre)
    in_up = move(in_part[4].astype(half), dz=1)
    held_next, incoming_next = after((held_next, incoming_next), in_part[4])
    in_part[2], held_next, incoming_next = after((in_part[2], held_next, incoming_next))

    gain_next, weights_next, scales_next, picked_next = small
    for step in range(3):
        out_up, in_down = after((out_up, in_down), in_part[4])
        if step < 2:
            out_up, in_down = add(out_part[6 + step], out_up), add(in_part[2 - step], in_down)
            out_down, in_up = after((out_down, in_up), out_up, in_down)
            out_up, in_down = move(out_up, dz=1), move(in_down, dz=-1)
        else:
            out_rest = out_part[0] + out_up.astype(f32)
            in_rest = in_part[0] + in_down.astype(f32)
            out_down, in_up = after((out_down, in_up), out_rest, in_rest)
        out_down, in_up = add(out_part[3 - step], out_down), add(in_part[5 + step], in_up)
        out_down, in_up = move(out_down, dz=-1), move(in_up, dz=1)
    out_sum = add(out_rest, out_down)
    in_sum = add(in_rest, in_up)
    out_slots = from_experts(out_sum, 1).astype(f32)
    in_slots = from_experts(in_sum, -1).astype(f32)

    lead = (((0,), (0,)), ((), ()))
    combined = lax.dot_general(
        weights_next, out_slots, lead, precision=lax.Precision.HIGHEST, preferred_element_type=f32
    )
    next_inputs = (held_next.astype(f32) + combined).astype(bf16)

    scale_next = jnp.sum(scales_next, axis=1, keepdims=True)
    from_x = picked_next.astype(f32)
    through = jnp.sum(from_x * gain_next * in_slots, axis=1, keepdims=True)
    change = scale_next * gain_next * in_slots - from_x * (scale_next * scale_next * scale_next) / width * through
    spread = lax.dot_general(
        (scales_next > 0).astype(f32), change, lead, precision=lax.Precision.HIGHEST, preferred_element_type=f32
    )
    prior_grads = (incoming_next.astype(f32) + spread).astype(bf16)
    return (next_inputs[None], prior_grads[None])


def solution(mesh):
    return jax.shard_map(
        on_device,
        mesh=mesh,
        in_specs=(
            P("pipe", "expert", None),
            P("pipe", "expert", None),
            P("pipe", "expert", None),
            P("pipe", "expert", None),
            P("pipe", None),
            P("pipe", None, "expert"),
            P("pipe", None, "expert"),
            P("pipe", "expert", None),
        ),
        out_specs=(P("pipe", "expert", None), P("pipe", "expert", None)),
        check_vma=False,
    )
```

```python
import jax
import jax.numpy as jnp
from jax import lax
from jax.experimental import pallas as pl
from jax.experimental.pallas import tpu as pltpu
from jax.sharding import PartitionSpec as P

EXP_WIN = 4
CAP = 6
EPSILON = 1e-06
NX, NZ, NC = 4, 8, 2
BOTH = ("pipe", "expert")
STRIPS = 7
PAD = 8
NOTE = 128
F32, BF16 = jnp.float32, jnp.bfloat16
LAST = (((1,), (1,)), ((), ()))
FIRST = (((0,), (0,)), ((), ()))
VMEM = pl.BlockSpec(memory_space=pltpu.VMEM)


def move(block, dy=0, dx=0, dz=0, dc=0):
    ny = lax.axis_size("pipe")
    route = []
    for y in range(ny):
        for x in range(NX):
            for z in range(NZ):
                for c in range(NC):
                    a = ((y * NX + x) * NZ + z) * NC + c
                    b = (((y + dy) % ny * NX + (x + dx) % NX) * NZ + (z + dz) % NZ) * NC + (c + dc) % NC
                    route.append((a, b))
    return lax.ppermute(block, BOTH, route)


def after(values, *needed):
    return lax.optimization_barrier((values, needed))[0]


def add(part, got):
    return (got.astype(F32) + part.astype(F32)).astype(BF16)


def product(a, b):
    return jnp.dot(a, b, preferred_element_type=F32)


def product_t(a, b):
    return lax.dot_general(a, b, LAST, preferred_element_type=F32)


def params(mib):
    return pltpu.CompilerParams(vmem_limit_bytes=mib * 2**20)


def three(value):
    high = value.astype(BF16).astype(F32)
    middle = (value - high).astype(BF16).astype(F32)
    return high, middle, value - high - middle


def strips(width):
    strip = width // STRIPS
    return [slice(s * strip, (s + 1) * strip) for s in range(STRIPS)]


def pick_kernel(column, routes, gates, held, incoming, *blocks):
    tokens, width = held.shape
    marks, weights = [], []
    for k in range(NX):
        named = routes[...] == lax.rem(column[0] + k, EXP_WIN)
        marks.append(jnp.max(named.astype(F32), axis=0, keepdims=True))
        weights.append(jnp.sum(jnp.where(named, gates[...], 0.0), axis=0, keepdims=True))
    before = lax.broadcasted_iota(jnp.int32, (tokens, tokens), 0)
    later = lax.broadcasted_iota(jnp.int32, (tokens, tokens), 1)
    order = (before < later).astype(BF16)
    slot = lax.broadcasted_iota(jnp.int32, (PAD, tokens), 0).astype(F32)
    token = lax.broadcasted_iota(jnp.int32, (PAD, tokens), 1).astype(F32) + 1.0
    picks, loads, notes = [], [], []
    lane = lax.broadcasted_iota(jnp.int32, (PAD, NOTE), 1)
    for k in range(NX):
        mark = jnp.broadcast_to(marks[k], (PAD, tokens))
        place = product(mark.astype(BF16), order)
        pick = jnp.where((place == slot) & (mark > 0.0), 1.0, 0.0)
        load = jnp.sum(pick * weights[k], axis=1, keepdims=True)
        which = jnp.sum(pick * token, axis=1, keepdims=True)
        note = jnp.where(lane == 0, which, 0.0)
        for i, piece in enumerate(three(load)):
            note = jnp.where(lane == i + 1, piece, note)
        picks.append(pick)
        loads.append(load)
        notes.append(note)
    pick = jnp.concatenate(picks, axis=0).astype(BF16)
    load = jnp.concatenate(loads, axis=0)
    for at in strips(width):
        rows = product(pick, held[:, at])
        grads = load * product(pick, incoming[:, at])
        for k in range(NX):
            mine = slice(k * PAD, (k + 1) * PAD)
            blocks[k][:, at] = rows[mine].astype(BF16)
            blocks[k][:, slice(width + at.start, width + at.stop)] = grads[mine].astype(BF16)
    for k in range(NX):
        blocks[k][:, 2 * width :] = notes[k].astype(BF16)


def pick_rows(column, routes, gates, held, incoming):
    width = held.shape[1]
    block = jax.ShapeDtypeStruct((PAD, 2 * width + NOTE), BF16)
    return pl.pallas_call(
        pick_kernel,
        out_shape=[block] * NX,
        in_specs=[pl.BlockSpec(memory_space=pltpu.SMEM)] + [VMEM] * 4,
        out_specs=[VMEM] * NX,
        compiler_params=params(16),
    )(column, routes, gates, held, incoming)


def packing(shape, dim):
    tall = lax.broadcasted_iota(jnp.int32, shape, dim)
    short = lax.broadcasted_iota(jnp.int32, shape, 1 - dim)
    block = short // CAP
    return (tall == block * PAD + (short - block * CAP)).astype(BF16)


def unpack_kernel(*refs):
    blocks, gain = refs[:NX], refs[NX]
    rows, grads, raw, facts = refs[NX + 1 :]
    width = gain.shape[1]
    pack = packing((NX * CAP, NX * PAD), 1)

    def compact(at):
        tall = jnp.concatenate([b[:, at].astype(F32) for b in blocks], axis=0)
        return product(pack, tall.astype(BF16))

    total = jnp.zeros((NX * CAP, 1), F32)
    for at in strips(width):
        part = compact(at)
        raw[:, at] = part.astype(BF16)
        total += jnp.sum(part * part, axis=1, keepdims=True)
    scale = lax.rsqrt(total / width + EPSILON)
    for at in strips(width):
        rows[:, at] = (raw[:, at].astype(F32) * scale * gain[:, at]).astype(BF16)
        grads[:, at] = compact(slice(width + at.start, width + at.stop)).astype(BF16)
    note = compact(slice(2 * width, 2 * width + NOTE))
    load = note[:, 1:2] + note[:, 2:3] + note[:, 3:4]
    lane = lax.broadcasted_iota(jnp.int32, note.shape, 1)
    facts[...] = jnp.where(lane == 0, note, jnp.where(lane == 1, load, scale))


def unpack(blocks, gain):
    width = gain.shape[1]
    chunk = jax.ShapeDtypeStruct((NX * CAP, width), BF16)
    facts = jax.ShapeDtypeStruct((NX * CAP, NOTE), F32)
    return pl.pallas_call(
        unpack_kernel,
        out_shape=[chunk, chunk, chunk, facts],
        in_specs=[VMEM] * (NX + 1),
        out_specs=[VMEM] * 4,
        compiler_params=params(16),
    )(*blocks, gain)


def spread(blocks, value, at):
    tall = product(packing((NX * PAD, NX * CAP), 0), value.astype(BF16))
    for k in range(NX):
        blocks[k][:, at] = tall[k * PAD : (k + 1) * PAD].astype(BF16)


def finish_out_kernel(part, above, below, facts, *blocks):
    width = part.shape[1]
    for at in strips(width):
        total = part[:, at].astype(F32) + above[:, at].astype(F32) + below[:, at].astype(F32)
        spread(blocks, facts[:, 1:2] * total, at)
    spread(blocks, facts[...], slice(width, width + NOTE))


def finish_in_kernel(part, above, below, facts, raw, gain, *refs):
    blocks, held = refs[:-1], refs[-1]
    width = part.shape[1]
    scale = facts[:, 2:3]
    through = jnp.zeros_like(scale)
    for at in strips(width):
        total = part[:, at].astype(F32) + above[:, at].astype(F32) + below[:, at].astype(F32)
        total = gain[:, at] * total
        held[:, at] = total
        through += jnp.sum(raw[:, at].astype(F32) * total, axis=1, keepdims=True)
    factor = scale * scale * scale / width * through
    for at in strips(width):
        spread(blocks, scale * held[:, at] - raw[:, at].astype(F32) * factor, at)
    spread(blocks, facts[...], slice(width, width + NOTE))


def finish(kernel, *given):
    high, width = given[0].shape
    scratch = [pltpu.VMEM((high, width), F32)] if kernel is finish_in_kernel else []
    return pl.pallas_call(
        kernel,
        out_shape=[jax.ShapeDtypeStruct((PAD, width + NOTE), BF16)] * NX,
        in_specs=[VMEM] * len(given),
        out_specs=[VMEM] * NX,
        scratch_shapes=scratch,
        compiler_params=params(16),
    )(*given)


def merge_kernel(base, *refs):
    rows, notes, out = refs[:NX], refs[NX : 2 * NX], refs[2 * NX]
    tokens = base.shape[0]
    which = jnp.concatenate([n[...].astype(F32)[:, 0:1] for n in notes], axis=0)
    token = lax.broadcasted_iota(jnp.int32, (NX * PAD, tokens), 1).astype(F32) + 1.0
    pick = (which == token).astype(BF16)
    tall = jnp.concatenate([r[...].astype(F32) for r in rows], axis=0).astype(BF16)
    more = lax.dot_general(pick, tall, FIRST, preferred_element_type=F32)
    out[...] = (base[...].astype(F32) + more).astype(BF16)


def merge(base, blocks):
    tokens, width = base.shape
    strip = width // STRIPS
    return pl.pallas_call(
        merge_kernel,
        grid=(STRIPS,),
        out_shape=jax.ShapeDtypeStruct(base.shape, BF16),
        in_specs=[pl.BlockSpec((tokens, strip), lambda i: (0, i))]
        + [pl.BlockSpec((PAD, strip), lambda i: (0, i))] * NX
        + [pl.BlockSpec((PAD, NOTE), lambda i: (0, width // NOTE))] * NX,
        out_specs=pl.BlockSpec((tokens, strip), lambda i: (0, i)),
        compiler_params=params(16),
    )(base, *blocks, *blocks)


def experts_kernel(count, forward, backward, *refs):
    refs = list(refs)
    take = lambda n: [refs.pop(0) for _ in range(n)]
    rows = take(count) if forward else []
    grads = take(count) if backward else []
    pre_in = take(0 if forward else 2)
    gates, ups, downs = take(NC), take(NC), take(NC)
    outs = take(count) if forward else []
    ins = take(count) if backward else []
    pre_out = take(0 if backward else 2)
    width = downs[0].shape[1]
    each = downs[0].shape[0]
    high = (rows or grads)[0].shape[0]
    cores = range(NC)

    def stack(blocks, at):
        if len(blocks) == 1:
            return blocks[0][:, at]
        return jnp.concatenate([b[:, at].astype(F32) for b in blocks], axis=0).astype(BF16)

    zero = [jnp.zeros((count * high, each), F32)] * NC
    gate_pre, up_pre, hidden_grad = list(zero), list(zero), list(zero)
    if not forward:
        gate_pre = [pre_in[0][:, c * each : (c + 1) * each] for c in cores]
        up_pre = [pre_in[1][:, c * each : (c + 1) * each] for c in cores]
    for at in strips(width):
        if forward:
            here = stack(rows, at)
            for c in cores:
                gate_pre[c] += product(here, gates[c][at, :])
                up_pre[c] += product(here, ups[c][at, :])
        if backward:
            here = stack(grads, at)
            for c in cores:
                hidden_grad[c] += product_t(here, downs[c][:, at])
    hidden, gate_grad, up_grad = [], [], []
    for c in cores:
        sigma = jax.nn.sigmoid(gate_pre[c])
        silu = gate_pre[c] * sigma
        if not backward:
            pre_out[0][:, c * each : (c + 1) * each] = gate_pre[c]
            pre_out[1][:, c * each : (c + 1) * each] = up_pre[c]
        hidden.append((silu * up_pre[c]).astype(BF16))
        slope = sigma * (1.0 + gate_pre[c] * (1.0 - sigma))
        gate_grad.append((hidden_grad[c] * up_pre[c] * slope).astype(BF16))
        up_grad.append((hidden_grad[c] * silu).astype(BF16))
    for at in strips(width):
        if forward:
            got = sum(product(hidden[c], downs[c][:, at]) for c in cores).astype(BF16)
            for i in range(count):
                outs[i][:, at] = got[i * high : (i + 1) * high]
        if backward:
            got = sum(product_t(gate_grad[c], gates[c][at, :]) for c in cores)
            got = (got + sum(product_t(up_grad[c], ups[c][at, :]) for c in cores)).astype(BF16)
            for i in range(count):
                ins[i][:, at] = got[i * high : (i + 1) * high]


def experts(rows, grads, weights, pre=None):
    forward, backward = bool(rows), bool(grads)
    count = max(len(rows), len(grads))
    high, width = (rows or grads)[0].shape
    units = NC * weights[0].shape[1]
    shapes = [jax.ShapeDtypeStruct((high, width), BF16)] * (len(rows) + len(grads))
    if not backward:
        shapes += [jax.ShapeDtypeStruct((count * high, units), F32)] * 2
    given = [*rows, *grads] + ([] if forward else list(pre))
    passes = 3 * (forward + backward)
    return pl.pallas_call(
        lambda *refs: experts_kernel(count, forward, backward, *refs),
        out_shape=shapes,
        in_specs=[VMEM] * (len(given) + 6),
        out_specs=[VMEM] * len(shapes),
        compiler_params=params(28),
        cost_estimate=pl.CostEstimate(
            flops=2 * passes * count * high * width * units, bytes_accessed=6 * width * units, transcendentals=0
        ),
    )(*given, *weights)


def on_device(inputs, out_grads, routes, gates, norm_gain, w_gate, w_up, w_down):
    held, incoming = inputs[0], out_grads[0]
    column = (lax.axis_index("expert") // (NZ * NC)).astype(jnp.int32).reshape(1)
    own = (w_gate[0], w_up[0], w_down[0])
    swapped = [move(w, dc=1) for w in own]
    incoming_next, held_next = move(incoming, dy=-1), move(held, dy=1)
    blocks = pick_rows(column, routes[0].T, gates[0].T, held, incoming)
    blocks, swapped = after((blocks, swapped))
    blocks = [blocks[0]] + [move(blocks[k], dx=k) for k in range(1, NX)]
    first_rows, first_grads, raw, facts = unpack(blocks, norm_gain)

    first_rows, first_grads, swapped = after((first_rows, first_grads, swapped))
    rows, grads = {0: first_rows}, {0: first_grads}
    rows[1], rows[7] = move(rows[0], dz=1), move(rows[0], dz=-1)
    grads[1], grads[7] = move(grads[0], dz=1), move(grads[0], dz=-1)

    rows[1], rows[7] = after((rows[1], rows[7]))
    rows[2], rows[6] = move(rows[1], dz=1), move(rows[7], dz=-1)
    grads[1], grads[7] = after((grads[1], grads[7]))
    grads[2], grads[6] = move(grads[1], dz=1), move(grads[7], dz=-1)

    out_part, in_part = {}, {}
    rows[2], rows[6], incoming_next, held_next = after((rows[2], rows[6], incoming_next, held_next))
    weights = [own[0], swapped[0], own[1], swapped[1], own[2], swapped[2]]

    def work(group, *needed):
        mine = after(([rows[j] for j in group], [grads[j] for j in group]), *needed)
        got = experts(mine[0], mine[1], weights)
        for i, j in enumerate(group):
            out_part[j], in_part[j] = got[i], got[len(group) + i]

    rows[3], rows[5] = move(rows[2], dz=1), move(rows[6], dz=-1)
    grads[2], grads[6] = after((grads[2], grads[6]))
    grads[3], grads[5] = move(grads[2], dz=1), move(grads[6], dz=-1)

    work((0, 1, 7, 2, 6))
    rows[3], rows[5] = after((rows[3], rows[5]), out_part[0])
    rows[4] = move(rows[3], dz=1)
    grads[3], grads[5] = after((grads[3], grads[5]))
    grads[4] = move(grads[5], dz=-1)

    work((3, 5))
    out_up = move(out_part[5], dz=1)
    in_down = move(in_part[3], dz=-1)
    rows[4] = after(rows[4], out_part[3])
    out_part[4], *pre = experts([rows[4]], [], weights)
    out_down = move(out_part[4], dz=-1)
    grads[4] = after(grads[4], out_part[4])
    (in_part[4],) = experts([], [grads[4]], weights, pre)
    in_up = move(in_part[4], dz=1)

    for step in range(2):
        out_up, in_down = after((out_up, in_down), in_part[4])
        out_up, in_down = add(out_part[6 + step], out_up), add(in_part[2 - step], in_down)
        out_down, in_up = after((out_down, in_up), out_up, in_down)
        out_up, in_down = move(out_up, dz=1), move(in_down, dz=-1)
        out_down, in_up = add(out_part[3 - step], out_down), add(in_part[5 + step], in_up)
        out_down, in_up = move(out_down, dz=-1), move(in_up, dz=1)
    out_down, in_up = add(out_part[1], out_down), add(in_part[7], in_up)
    out_down, in_up = move(out_down, dz=-1), move(in_up, dz=1)

    blocks = finish(finish_out_kernel, out_part[0], out_up, out_down, facts)
    out_blocks = [move(blocks[k], dx=-k, dy=1) for k in range(NX)]
    blocks = finish(finish_in_kernel, in_part[0], in_up, in_down, facts, raw, norm_gain)
    in_blocks = [move(blocks[k], dx=-k, dy=-1) for k in range(NX)]
    next_inputs = merge(held_next, out_blocks)
    prior_grads = merge(incoming_next, in_blocks)
    return (next_inputs[None], prior_grads[None])


def solution(mesh):
    return jax.shard_map(
        on_device,
        mesh=mesh,
        in_specs=(
            P("pipe", "expert", None),
            P("pipe", "expert", None),
            P("pipe", "expert", None),
            P("pipe", "expert", None),
            P("pipe", None),
            P("pipe", None, "expert"),
            P("pipe", None, "expert"),
            P("pipe", "expert", None),
        ),
        out_specs=(P("pipe", "expert", None), P("pipe", "expert", None)),
        check_vma=False,
    )
```

```python
import jax
import jax.numpy as jnp
from jax import lax
from jax.experimental import pallas as pl
from jax.experimental.pallas import tpu as pltpu
from jax.sharding import PartitionSpec as P

EXP_WIN = 4
CAP = 6
EPSILON = 1e-06
NX, NZ, NC = 4, 8, 2
BOTH = ("pipe", "expert")
STRIPS = 7
FOLDS = 4
PICK_MIB = 52
ROWS = NX * FOLDS * CAP
NOTE = 128
F32, BF16 = jnp.float32, jnp.bfloat16
LAST = (((1,), (1,)), ((), ()))
FIRST = (((0,), (0,)), ((), ()))
VMEM = pl.BlockSpec(memory_space=pltpu.VMEM)
ANY = pl.BlockSpec(memory_space=pl.ANY)


def move(block, dy=0, dx=0, dz=0, dc=0):
    ny = lax.axis_size("pipe")
    route = []
    for y in range(ny):
        for x in range(NX):
            for z in range(NZ):
                for c in range(NC):
                    a = ((y * NX + x) * NZ + z) * NC + c
                    b = (((y + dy) % ny * NX + (x + dx) % NX) * NZ + (z + dz) % NZ) * NC + (c + dc) % NC
                    route.append((a, b))
    return lax.ppermute(block, BOTH, route)


def after(values, *needed):
    return lax.optimization_barrier((values, needed))[0]


def add(part, got):
    return (got.astype(F32) + part.astype(F32)).astype(BF16)


def product(a, b):
    return jnp.dot(a, b, preferred_element_type=F32)


def product_t(a, b):
    return lax.dot_general(a, b, LAST, preferred_element_type=F32)


def params(mib):
    return pltpu.CompilerParams(vmem_limit_bytes=mib * 2**20)


def three(value):
    high = value.astype(BF16).astype(F32)
    middle = (value - high).astype(BF16).astype(F32)
    return high, middle, value - high - middle


def strips(width):
    strip = width // STRIPS
    return [slice(s * strip, (s + 1) * strip) for s in range(STRIPS)]


def copy_in(sources, targets, sems):
    copies = [pltpu.make_async_copy(a, b, sems.at[i]) for i, (a, b) in enumerate(zip(sources, targets))]
    for copy in copies:
        copy.start()
    return copies


def folds(width):
    fold = width // FOLDS
    strip = fold // 2
    for s in range(2):
        here = slice(s * strip, (s + 1) * strip)
        yield here, [slice(q * fold + here.start, q * fold + here.stop) for q in range(FOLDS)]


def row_parts(shape, dim):
    row = lax.broadcasted_iota(jnp.int32, shape, dim)
    block = row // (FOLDS * CAP)
    rest = row - block * (FOLDS * CAP)
    fold = rest // CAP
    return block, fold, rest - fold * CAP


def folding(q, dim):
    shape = (ROWS, NX * CAP) if dim == 0 else (NX * CAP, ROWS)
    block, fold, slot = row_parts(shape, dim)
    short = lax.broadcasted_iota(jnp.int32, shape, 1 - dim)
    hit = short == block * CAP + slot
    if q is not None:
        hit = hit & (fold == q)
    return hit.astype(F32).astype(BF16)


def pick_kernel(column, *refs):
    blocks = refs[4 : 4 + NX]
    routes, gates, held, incoming, sems = refs[4 + NX :]
    tokens, width = held.shape
    ids_in, gates_in, *loads_in = copy_in(refs[:4], (routes, gates, held, incoming), sems)
    before = lax.broadcasted_iota(jnp.int32, (tokens, tokens), 0)
    later = lax.broadcasted_iota(jnp.int32, (tokens, tokens), 1)
    order = (before < later).astype(F32).astype(BF16)
    high = FOLDS * CAP
    shape = (high, tokens)
    slot = row_parts(shape, 0)[2].astype(F32)
    token = lax.broadcasted_iota(jnp.int32, shape, 1).astype(F32) + 1.0
    lane = lax.broadcasted_iota(jnp.int32, (high, NOTE), 1)
    picks, loads = [], []
    ids_in.wait()
    gates_in.wait()
    for k in range(NX):
        named = routes[...] == lax.rem(column[0] + k, EXP_WIN)
        mark = jnp.max(named.astype(F32), axis=0, keepdims=True)
        weight = jnp.sum(jnp.where(named, gates[...], 0.0), axis=0, keepdims=True)
        mark = jnp.broadcast_to(mark, shape)
        place = product(mark.astype(BF16), order)
        pick = jnp.where((place == slot) & (mark > 0.0), 1.0, 0.0)
        load = jnp.sum(pick * weight, axis=1, keepdims=True)
        which = jnp.sum(pick * token, axis=1, keepdims=True)
        note = jnp.where(lane == 0, which, 0.0)
        for i, piece in enumerate(three(load)):
            note = jnp.where(lane == i + 1, piece, note)
        blocks[k][:, 2 * width // FOLDS :] = note.astype(BF16)
        picks.append(pick)
        loads.append(load)
    pick = jnp.concatenate(picks, axis=0)
    load = jnp.concatenate(loads, axis=0)
    fold = row_parts((ROWS, tokens), 0)[1]
    parts = [jnp.where(fold == q, pick, 0.0).astype(BF16) for q in range(FOLDS)]
    for i, source in enumerate((held, incoming)):
        loads_in[i].wait()
        for here, plain in folds(width):
            got = sum(product(parts[q], source[:, plain[q]]) for q in range(FOLDS))
            got = (load * got if i else got).astype(BF16)
            for k in range(NX):
                at = slice(i * width // FOLDS + here.start, i * width // FOLDS + here.stop)
                blocks[k][:, at] = got[k * high : (k + 1) * high]


def pick_rows(column, routes, gates, held, incoming):
    tokens, width = held.shape
    high, fold = FOLDS * CAP, width // FOLDS
    return pl.pallas_call(
        pick_kernel,
        out_shape=[jax.ShapeDtypeStruct((high, 2 * fold + NOTE), BF16)] * NX,
        in_specs=[pl.BlockSpec(memory_space=pltpu.SMEM)] + [ANY] * 4,
        out_specs=[VMEM] * NX,
        scratch_shapes=[
            pltpu.VMEM(routes.shape, routes.dtype),
            pltpu.VMEM(gates.shape, gates.dtype),
            pltpu.VMEM((tokens, width), BF16),
            pltpu.VMEM((tokens, width), BF16),
            pltpu.SemaphoreType.DMA((4,)),
        ],
        compiler_params=params(PICK_MIB),
    )(column, routes, gates, held, incoming)


def stacked(blocks, at):
    return jnp.concatenate([b[:, at].astype(F32) for b in blocks], axis=0).astype(BF16)


def unfold_kernel(*refs):
    blocks, gain = refs[:NX], refs[NX]
    pair, raw, facts = refs[NX + 1 :]
    width = gain.shape[1]
    total = jnp.zeros((NX * CAP, 1), F32)
    turns = [folding(q, 1) for q in range(FOLDS)]
    for here, plain in folds(width):
        tall = stacked(blocks, here)
        for q in range(FOLDS):
            part = product(turns[q], tall)
            raw[:, plain[q]] = part.astype(BF16)
            total += jnp.sum(part * part, axis=1, keepdims=True)
    scale = lax.rsqrt(total / width + EPSILON)
    for at in strips(width):
        pair[0, :, at] = (raw[:, at].astype(F32) * scale * gain[:, at]).astype(BF16)
    for here, plain in folds(width):
        tall = stacked(blocks, slice(width // FOLDS + here.start, width // FOLDS + here.stop))
        for q in range(FOLDS):
            pair[1, :, plain[q]] = product(turns[q], tall).astype(BF16)
    note = product(turns[0], stacked(blocks, slice(2 * width // FOLDS, 2 * width // FOLDS + NOTE)))
    load = note[:, 1:2] + note[:, 2:3] + note[:, 3:4]
    lane = lax.broadcasted_iota(jnp.int32, note.shape, 1)
    facts[...] = jnp.where(lane == 0, note, jnp.where(lane == 1, load, scale))


def unfold(blocks, gain):
    width = gain.shape[1]
    chunk = jax.ShapeDtypeStruct((NX * CAP, width), BF16)
    facts = jax.ShapeDtypeStruct((NX * CAP, NOTE), F32)
    return pl.pallas_call(
        unfold_kernel,
        out_shape=[jax.ShapeDtypeStruct((2, *chunk.shape), BF16), chunk, facts],
        in_specs=[VMEM] * (NX + 1),
        out_specs=[VMEM] * 3,
        compiler_params=params(8),
    )(*blocks, gain)


def fold_out(blocks, facts, width, value):
    high = FOLDS * CAP
    turns = [folding(q, 0) for q in range(FOLDS)]
    for here, plain in folds(width):
        tall = sum(product(turns[q], value(plain[q]).astype(BF16)) for q in range(FOLDS)).astype(BF16)
        for k in range(NX):
            blocks[k][:, here] = tall[k * high : (k + 1) * high]
    tall = product(folding(None, 0), facts[...].astype(BF16)).astype(BF16)
    for k in range(NX):
        blocks[k][:, width // FOLDS :] = tall[k * high : (k + 1) * high]


def finish_out_kernel(part, above, below, facts, *blocks):
    def value(at):
        total = part[:, at].astype(F32) + above[:, at].astype(F32) + below[:, at].astype(F32)
        return facts[:, 1:2] * total

    fold_out(blocks, facts, part.shape[1], value)


def finish_in_kernel(part, above, below, facts, raw, gain, *refs):
    blocks, held = refs[:-1], refs[-1]
    width = part.shape[1]
    scale = facts[:, 2:3]
    through = jnp.zeros_like(scale)
    for at in strips(width):
        total = part[:, at].astype(F32) + above[:, at].astype(F32) + below[:, at].astype(F32)
        total = gain[:, at] * total
        held[:, at] = total
        through += jnp.sum(raw[:, at].astype(F32) * total, axis=1, keepdims=True)
    factor = scale * scale * scale / width * through
    fold_out(blocks, facts, width, lambda at: scale * held[:, at] - raw[:, at].astype(F32) * factor)


def finish(kernel, *given):
    high, width = given[0].shape
    scratch = [pltpu.VMEM((high, width), F32)] if kernel is finish_in_kernel else []
    return pl.pallas_call(
        kernel,
        out_shape=[jax.ShapeDtypeStruct((FOLDS * CAP, width // FOLDS + NOTE), BF16)] * NX,
        in_specs=[VMEM] * len(given),
        out_specs=[VMEM] * NX,
        scratch_shapes=scratch,
        compiler_params=params(8),
    )(*given)


def merge_kernel(count, *refs):
    bases, blocks, out_hbm = refs[:count], refs[count : count + NX], refs[count + NX]
    base, out, in_sems, out_sems = refs[count + NX + 1 :]
    tokens, width = base.shape
    fold = width // FOLDS
    spans = [pl.ds(q * fold, fold) for q in range(FOLDS)]
    sources, targets = [], []
    for at in spans:
        top = 0
        for part in bases:
            high = part.shape[0]
            sources.append(part.at[:, at])
            targets.append(base.at[pl.ds(top, high), at])
            top += high
    loads = copy_in(sources, targets, in_sems)
    which = jnp.concatenate([b[:, fold:].astype(F32)[:, 0:1] for b in blocks], axis=0)
    token = lax.broadcasted_iota(jnp.int32, (ROWS, tokens), 1).astype(F32) + 1.0
    part = row_parts((ROWS, tokens), 0)[1]
    stores = []
    for q in range(FOLDS):
        pick = jnp.where((which == token) & (part == q), 1.0, 0.0).T.astype(BF16)
        for copy in loads[q * count : (q + 1) * count]:
            copy.wait()
        for half in range(2):
            here = slice(half * fold // 2, (half + 1) * fold // 2)
            at = slice(q * fold + here.start, q * fold + here.stop)
            more = product(pick, stacked(blocks, here))
            out[:, at] = (base[:, at].astype(F32) + more).astype(BF16)
        copy = pltpu.make_async_copy(out.at[:, spans[q]], out_hbm.at[:, spans[q]], out_sems.at[q])
        copy.start()
        stores.append(copy)
    for copy in stores:
        copy.wait()


def merge(bases, blocks):
    tokens, width = sum(b.shape[0] for b in bases), bases[0].shape[1]
    count = len(bases)
    return pl.pallas_call(
        lambda *refs: merge_kernel(count, *refs),
        out_shape=jax.ShapeDtypeStruct((tokens, width), BF16),
        in_specs=[ANY] * count + [VMEM] * NX,
        out_specs=ANY,
        scratch_shapes=[pltpu.VMEM((tokens, width), BF16)] * 2
        + [pltpu.SemaphoreType.DMA((FOLDS * count,)), pltpu.SemaphoreType.DMA((FOLDS,))],
        compiler_params=params(8),
    )(*bases, *blocks)


def stage_kernel(*refs):
    sources, (gate_w, up_w, down_w, sems) = refs[:6], refs[6:]
    each = sources[4].shape[0]
    targets = []
    for i, wide in enumerate((gate_w, up_w, down_w)):
        for core in range(NC):
            span = pl.ds(core * each, each)
            targets.append(wide.at[span, :] if i == 2 else wide.at[:, span])
    for copy in copy_in(sources, targets, sems):
        copy.wait()


def stage(own, swapped):
    width, each = own[0].shape
    tall = jax.ShapeDtypeStruct((width, NC * each), BF16)
    wide = jax.ShapeDtypeStruct((NC * each, width), BF16)
    return pl.pallas_call(
        stage_kernel,
        out_shape=[tall, tall, wide],
        in_specs=[ANY] * 6,
        out_specs=[VMEM] * 3,
        scratch_shapes=[pltpu.SemaphoreType.DMA((6,))],
        compiler_params=params(16),
    )(own[0], swapped[0], own[1], swapped[1], own[2], swapped[2])


def experts_kernel(paired, count, forward, backward, *refs):
    refs = list(refs)
    take = lambda n: [refs.pop(0) for _ in range(n)]
    pairs = take(paired)
    rows = [p.at[0] for p in pairs] + take(count - paired if forward else 0)
    grads = [p.at[1] for p in pairs] + take(count - paired if backward else 0)
    pre_in = take(0 if forward else 2)
    gate_w, up_w, down_w = take(3)
    outs = take(count) if forward else []
    ins = take(count) if backward else []
    pre_out = take(0 if backward else 2)
    units, width = down_w.shape
    high = (rows or grads)[0].shape[0]

    def stack(blocks, at):
        if len(blocks) == 1:
            return blocks[0][:, at]
        return stacked(blocks, at)

    gate_pre = up_pre = hidden_grad = jnp.zeros((count * high, units), F32)
    if not forward:
        gate_pre, up_pre = pre_in[0][...], pre_in[1][...]
    for at in strips(width):
        if forward:
            here = stack(rows, at)
            gate_pre += product(here, gate_w[at, :])
            up_pre += product(here, up_w[at, :])
        if backward:
            hidden_grad += product_t(stack(grads, at), down_w[:, at])
    sigma = jax.nn.sigmoid(gate_pre)
    silu = gate_pre * sigma
    if not backward:
        pre_out[0][...] = gate_pre
        pre_out[1][...] = up_pre
    hidden = (silu * up_pre).astype(BF16)
    slope = sigma * (1.0 + gate_pre * (1.0 - sigma))
    gate_grad = (hidden_grad * up_pre * slope).astype(BF16)
    up_grad = (hidden_grad * silu).astype(BF16)
    for at in strips(width):
        if forward:
            got = product(hidden, down_w[:, at])
            for i in range(count):
                outs[i][:, at] = got[i * high : (i + 1) * high].astype(BF16)
        if backward:
            got = product_t(gate_grad, gate_w[at, :]) + product_t(up_grad, up_w[at, :])
            for i in range(count):
                ins[i][:, at] = got[i * high : (i + 1) * high].astype(BF16)


def experts(pairs, rows, grads, weights, pre=()):
    forward, backward = bool(pairs or rows), bool(pairs or grads)
    count = len(pairs) + max(len(rows), len(grads))
    units, width = weights[2].shape
    high = NX * CAP
    shapes = [jax.ShapeDtypeStruct((high, width), BF16)] * (count * (forward + backward))
    if not backward:
        shapes += [jax.ShapeDtypeStruct((count * high, units), F32)] * 2
    given = [*pairs, *rows, *grads, *pre]
    passes = 3 * (forward + backward)
    return pl.pallas_call(
        lambda *refs: experts_kernel(len(pairs), count, forward, backward, *refs),
        out_shape=shapes,
        in_specs=[VMEM] * (len(given) + 3),
        out_specs=[VMEM] * len(shapes),
        compiler_params=params(16),
        cost_estimate=pl.CostEstimate(
            flops=2 * passes * count * high * width * units, bytes_accessed=6 * width * units, transcendentals=0
        ),
    )(*given, *weights)


def on_device(inputs, out_grads, routes, gates, norm_gain, w_gate, w_up, w_down):
    held, incoming = inputs[0], out_grads[0]
    column = (lax.axis_index("expert") // (NZ * NC)).astype(jnp.int32).reshape(1)
    own = (w_gate[0], w_up[0], w_down[0])
    swapped = [move(w, dc=1) for w in own]
    blocks = pick_rows(column, routes[0].T, gates[0].T, held, incoming)
    blocks, swapped[0] = after((blocks, swapped[0]))
    arrived = [blocks[0]] + [move(blocks[k], dx=k) for k in range(1, NX)]
    arrived, weights = after((arrived, stage(own, swapped)))
    first, raw, facts = unfold(arrived, norm_gain)

    held_next, incoming_next = [], []
    cuts = [0, 48, 96, held.shape[0]]
    pairs = {0: first, 1: move(first, dz=1), 7: move(first, dz=-1)}
    out_part, in_part = {}, {}

    def work(group):
        got = experts([pairs[j] for j in group], [], [], weights)
        for i, j in enumerate(group):
            out_part[j], in_part[j] = got[i], got[len(group) + i]

    for step in range(3):
        span = slice(cuts[step], cuts[step + 1])
        cut = (held[span], incoming[span])
        cut = after(cut, *(blocks if step == 0 else (pairs[step], pairs[NZ - step])))
        if step > 0:
            pairs[step + 1] = move(pairs[step], dz=1)
            pairs[NZ - step - 1] = move(pairs[NZ - step], dz=-1)
        passed = (move(cut[0], dy=1), move(cut[1], dy=-1))
        if step == 2:
            work((0, 1, 7, 2, 6))
        new = (pairs[step + 1], pairs[NZ - step - 1])
        (pairs[step + 1], pairs[NZ - step - 1]), passed = after((new, passed), out_part)
        held_next.append(passed[0])
        incoming_next.append(passed[1])

    last_rows, last_grads = move(pairs[3][0], dz=1), move(pairs[5][1], dz=-1)
    work((3, 5))
    out_up = move(out_part[5], dz=1)
    in_down = move(in_part[3], dz=-1)
    last_rows = after(last_rows, out_part[3])
    out_part[4], *pre = experts([], [last_rows], [], weights)
    out_down = move(out_part[4], dz=-1)
    last_grads = after(last_grads, out_part[4])
    (in_part[4],) = experts([], [], [last_grads], weights, pre)
    in_up = move(in_part[4], dz=1)

    for step in range(2):
        out_up, in_down = after((out_up, in_down), in_part[4])
        out_up, in_down = add(out_part[6 + step], out_up), add(in_part[2 - step], in_down)
        out_down, in_up = after((out_down, in_up), out_up, in_down)
        out_up, in_down = move(out_up, dz=1), move(in_down, dz=-1)
        out_down, in_up = add(out_part[3 - step], out_down), add(in_part[5 + step], in_up)
        out_down, in_up = move(out_down, dz=-1), move(in_up, dz=1)
    out_down, in_up = add(out_part[1], out_down), add(in_part[7], in_up)
    out_down, in_up = move(out_down, dz=-1), move(in_up, dz=1)

    blocks = finish(finish_out_kernel, out_part[0], out_up, out_down, facts)
    out_blocks = [move(blocks[k], dx=-k, dy=1) for k in range(NX)]
    blocks = finish(finish_in_kernel, in_part[0], in_up, in_down, facts, raw, norm_gain)
    in_blocks = [move(blocks[k], dx=-k, dy=-1) for k in range(NX)]
    next_inputs = merge(held_next, out_blocks)
    prior_grads = merge(incoming_next, in_blocks)
    return (next_inputs[None], prior_grads[None])


def solution(mesh):
    return jax.shard_map(
        on_device,
        mesh=mesh,
        in_specs=(
            P("pipe", "expert", None),
            P("pipe", "expert", None),
            P("pipe", "expert", None),
            P("pipe", "expert", None),
            P("pipe", None),
            P("pipe", None, "expert"),
            P("pipe", None, "expert"),
            P("pipe", "expert", None),
        ),
        out_specs=(P("pipe", "expert", None), P("pipe", "expert", None)),
        check_vma=False,
    )
```

```python
import jax
import jax.numpy as jnp
from jax import lax
from jax.experimental import pallas as pl
from jax.experimental.pallas import tpu as pltpu
from jax.sharding import PartitionSpec as P

EXP_WIN = 4
CAP = 6
EPSILON = 1e-06
NX, NZ, NC = 4, 8, 2
BOTH = ("pipe", "expert")
STRIPS = 7
FOLDS = 4
PICK_MIB = 52
FARTHEST = (2, 3, 1, 0)
PASSED_BY = 2
ROWS = NX * FOLDS * CAP
NOTE = 128
F32, BF16 = jnp.float32, jnp.bfloat16
LAST = (((1,), (1,)), ((), ()))
FIRST = (((0,), (0,)), ((), ()))
VMEM = pl.BlockSpec(memory_space=pltpu.VMEM)
ANY = pl.BlockSpec(memory_space=pl.ANY)


def move(block, dy=0, dx=0, dz=0, dc=0):
    ny = lax.axis_size("pipe")
    route = []
    for y in range(ny):
        for x in range(NX):
            for z in range(NZ):
                for c in range(NC):
                    a = ((y * NX + x) * NZ + z) * NC + c
                    b = (((y + dy) % ny * NX + (x + dx) % NX) * NZ + (z + dz) % NZ) * NC + (c + dc) % NC
                    route.append((a, b))
    return lax.ppermute(block, BOTH, route)


def after(values, *needed):
    return lax.optimization_barrier((values, needed))[0]


def add(part, got):
    return (got.astype(F32) + part.astype(F32)).astype(BF16)


def product(a, b):
    return jnp.dot(a, b, preferred_element_type=F32)


def product_t(a, b):
    return lax.dot_general(a, b, LAST, preferred_element_type=F32)


def params(mib):
    return pltpu.CompilerParams(vmem_limit_bytes=mib * 2**20)


def three(value):
    high = value.astype(BF16).astype(F32)
    middle = (value - high).astype(BF16).astype(F32)
    return high, middle, value - high - middle


def strips(width):
    strip = width // STRIPS
    return [slice(s * strip, (s + 1) * strip) for s in range(STRIPS)]


def copy_in(sources, targets, sems):
    copies = [pltpu.make_async_copy(a, b, sems.at[i]) for i, (a, b) in enumerate(zip(sources, targets))]
    for copy in copies:
        copy.start()
    return copies


def folds(width):
    fold = width // FOLDS
    strip = fold // 2
    for s in range(2):
        here = slice(s * strip, (s + 1) * strip)
        yield here, [slice(q * fold + here.start, q * fold + here.stop) for q in range(FOLDS)]


def row_parts(shape, dim):
    row = lax.broadcasted_iota(jnp.int32, shape, dim)
    block = row // (FOLDS * CAP)
    rest = row - block * (FOLDS * CAP)
    fold = rest // CAP
    return block, fold, rest - fold * CAP


def folding(q, dim):
    shape = (ROWS, NX * CAP) if dim == 0 else (NX * CAP, ROWS)
    block, fold, slot = row_parts(shape, dim)
    short = lax.broadcasted_iota(jnp.int32, shape, 1 - dim)
    hit = short == block * CAP + slot
    if q is not None:
        hit = hit & (fold == q)
    return hit.astype(F32).astype(BF16)


def pick_kernel(column, *refs):
    blocks = refs[4 : 4 + NX]
    routes, gates, held, incoming, sems = refs[4 + NX :]
    tokens, width = held.shape
    ids_in, gates_in, *loads_in = copy_in(refs[:4], (routes, gates, held, incoming), sems)
    before = lax.broadcasted_iota(jnp.int32, (tokens, tokens), 0)
    later = lax.broadcasted_iota(jnp.int32, (tokens, tokens), 1)
    order = (before < later).astype(F32).astype(BF16)
    high = FOLDS * CAP
    shape = (high, tokens)
    slot = row_parts(shape, 0)[2].astype(F32)
    token = lax.broadcasted_iota(jnp.int32, shape, 1).astype(F32) + 1.0
    lane = lax.broadcasted_iota(jnp.int32, (high, NOTE), 1)
    picks, loads = [], []
    ids_in.wait()
    gates_in.wait()
    for k in range(NX):
        named = routes[...] == lax.rem(column[0] + k, EXP_WIN)
        mark = jnp.max(named.astype(F32), axis=0, keepdims=True)
        weight = jnp.sum(jnp.where(named, gates[...], 0.0), axis=0, keepdims=True)
        mark = jnp.broadcast_to(mark, shape)
        place = product(mark.astype(BF16), order)
        pick = jnp.where((place == slot) & (mark > 0.0), 1.0, 0.0)
        load = jnp.sum(pick * weight, axis=1, keepdims=True)
        which = jnp.sum(pick * token, axis=1, keepdims=True)
        note = jnp.where(lane == 0, which, 0.0)
        for i, piece in enumerate(three(load)):
            note = jnp.where(lane == i + 1, piece, note)
        blocks[k][:, 2 * width // FOLDS :] = note.astype(BF16)
        picks.append(pick)
        loads.append(load)
    pick = jnp.concatenate(picks, axis=0)
    load = jnp.concatenate(loads, axis=0)
    fold = row_parts((ROWS, tokens), 0)[1]
    parts = [jnp.where(fold == q, pick, 0.0).astype(BF16) for q in range(FOLDS)]
    for i, source in enumerate((held, incoming)):
        loads_in[i].wait()
        for here, plain in folds(width):
            got = sum(product(parts[q], source[:, plain[q]]) for q in range(FOLDS))
            got = (load * got if i else got).astype(BF16)
            for k in range(NX):
                at = slice(i * width // FOLDS + here.start, i * width // FOLDS + here.stop)
                blocks[k][:, at] = got[k * high : (k + 1) * high]


def pick_rows(column, routes, gates, held, incoming):
    tokens, width = held.shape
    high, fold = FOLDS * CAP, width // FOLDS
    return pl.pallas_call(
        pick_kernel,
        out_shape=[jax.ShapeDtypeStruct((high, 2 * fold + NOTE), BF16)] * NX,
        in_specs=[pl.BlockSpec(memory_space=pltpu.SMEM)] + [ANY] * 4,
        out_specs=[VMEM] * NX,
        scratch_shapes=[
            pltpu.VMEM(routes.shape, routes.dtype),
            pltpu.VMEM(gates.shape, gates.dtype),
            pltpu.VMEM((tokens, width), BF16),
            pltpu.VMEM((tokens, width), BF16),
            pltpu.SemaphoreType.DMA((4,)),
        ],
        compiler_params=params(PICK_MIB),
    )(column, routes, gates, held, incoming)


def stacked(blocks, at):
    return jnp.concatenate([b[:, at].astype(F32) for b in blocks], axis=0).astype(BF16)


def unfold_kernel(*refs):
    blocks, gain = refs[:NX], refs[NX]
    pair, raw, facts = refs[NX + 1 :]
    width = gain.shape[1]
    total = jnp.zeros((NX * CAP, 1), F32)
    turns = [folding(q, 1) for q in range(FOLDS)]
    for here, plain in folds(width):
        tall = stacked(blocks, here)
        for q in range(FOLDS):
            part = product(turns[q], tall)
            raw[:, plain[q]] = part.astype(BF16)
            total += jnp.sum(part * part, axis=1, keepdims=True)
    scale = lax.rsqrt(total / width + EPSILON)
    for at in strips(width):
        pair[0, :, at] = (raw[:, at].astype(F32) * scale * gain[:, at]).astype(BF16)
    for here, plain in folds(width):
        tall = stacked(blocks, slice(width // FOLDS + here.start, width // FOLDS + here.stop))
        for q in range(FOLDS):
            pair[1, :, plain[q]] = product(turns[q], tall).astype(BF16)
    note = product(turns[0], stacked(blocks, slice(2 * width // FOLDS, 2 * width // FOLDS + NOTE)))
    load = note[:, 1:2] + note[:, 2:3] + note[:, 3:4]
    lane = lax.broadcasted_iota(jnp.int32, note.shape, 1)
    facts[...] = jnp.where(lane == 0, note, jnp.where(lane == 1, load, scale))


def unfold(blocks, gain):
    width = gain.shape[1]
    chunk = jax.ShapeDtypeStruct((NX * CAP, width), BF16)
    facts = jax.ShapeDtypeStruct((NX * CAP, NOTE), F32)
    return pl.pallas_call(
        unfold_kernel,
        out_shape=[jax.ShapeDtypeStruct((2, *chunk.shape), BF16), chunk, facts],
        in_specs=[VMEM] * (NX + 1),
        out_specs=[VMEM] * 3,
        compiler_params=params(8),
    )(*blocks, gain)


def fold_out(blocks, facts, width, value):
    high = FOLDS * CAP
    turns = [folding(q, 0) for q in range(FOLDS)]
    for here, plain in folds(width):
        tall = sum(product(turns[q], value(plain[q]).astype(BF16)) for q in range(FOLDS)).astype(BF16)
        for k in range(NX):
            blocks[k][:, here] = tall[k * high : (k + 1) * high]
    tall = product(folding(None, 0), facts[...].astype(BF16)).astype(BF16)
    for k in range(NX):
        blocks[k][:, width // FOLDS :] = tall[k * high : (k + 1) * high]


def finish_out_kernel(part, above, below, facts, *blocks):
    def value(at):
        total = part[:, at].astype(F32) + above[:, at].astype(F32) + below[:, at].astype(F32)
        return facts[:, 1:2] * total

    fold_out(blocks, facts, part.shape[1], value)


def finish_in_kernel(part, above, below, facts, raw, gain, *refs):
    blocks, held = refs[:-1], refs[-1]
    width = part.shape[1]
    scale = facts[:, 2:3]
    through = jnp.zeros_like(scale)
    for at in strips(width):
        total = part[:, at].astype(F32) + above[:, at].astype(F32) + below[:, at].astype(F32)
        total = gain[:, at] * total
        held[:, at] = total
        through += jnp.sum(raw[:, at].astype(F32) * total, axis=1, keepdims=True)
    factor = scale * scale * scale / width * through
    fold_out(blocks, facts, width, lambda at: scale * held[:, at] - raw[:, at].astype(F32) * factor)


def finish(kernel, *given):
    high, width = given[0].shape
    scratch = [pltpu.VMEM((high, width), F32)] if kernel is finish_in_kernel else []
    return pl.pallas_call(
        kernel,
        out_shape=[jax.ShapeDtypeStruct((FOLDS * CAP, width // FOLDS + NOTE), BF16)] * NX,
        in_specs=[VMEM] * len(given),
        out_specs=[VMEM] * NX,
        scratch_shapes=scratch,
        compiler_params=params(8),
    )(*given)


def merge_kernel(count, *refs):
    bases, blocks, out_hbm = refs[:count], refs[count : count + NX], refs[count + NX]
    base, out, in_sems, out_sems = refs[count + NX + 1 :]
    tokens, width = base.shape
    fold = width // FOLDS
    spans = [pl.ds(q * fold, fold) for q in range(FOLDS)]
    sources, targets = [], []
    for at in spans:
        top = 0
        for part in bases:
            high = part.shape[0]
            sources.append(part.at[:, at])
            targets.append(base.at[pl.ds(top, high), at])
            top += high
    loads = copy_in(sources, targets, in_sems)
    which = jnp.concatenate([b[:, fold:].astype(F32)[:, 0:1] for b in blocks], axis=0)
    token = lax.broadcasted_iota(jnp.int32, (ROWS, tokens), 1).astype(F32) + 1.0
    part = row_parts((ROWS, tokens), 0)[1]
    stores = []
    for q in range(FOLDS):
        pick = jnp.where((which == token) & (part == q), 1.0, 0.0).T.astype(BF16)
        for copy in loads[q * count : (q + 1) * count]:
            copy.wait()
        for half in range(2):
            here = slice(half * fold // 2, (half + 1) * fold // 2)
            at = slice(q * fold + here.start, q * fold + here.stop)
            more = product(pick, stacked(blocks, here))
            out[:, at] = (base[:, at].astype(F32) + more).astype(BF16)
        copy = pltpu.make_async_copy(out.at[:, spans[q]], out_hbm.at[:, spans[q]], out_sems.at[q])
        copy.start()
        stores.append(copy)
    for copy in stores:
        copy.wait()


def merge(bases, blocks):
    tokens, width = sum(b.shape[0] for b in bases), bases[0].shape[1]
    count = len(bases)
    return pl.pallas_call(
        lambda *refs: merge_kernel(count, *refs),
        out_shape=jax.ShapeDtypeStruct((tokens, width), BF16),
        in_specs=[ANY] * count + [VMEM] * NX,
        out_specs=ANY,
        scratch_shapes=[pltpu.VMEM((tokens, width), BF16)] * 2
        + [pltpu.SemaphoreType.DMA((FOLDS * count,)), pltpu.SemaphoreType.DMA((FOLDS,))],
        compiler_params=params(8),
    )(*bases, *blocks)


def stage_kernel(*refs):
    sources, (gate_w, up_w, down_w, sems) = refs[:6], refs[6:]
    each = sources[4].shape[0]
    targets = []
    for i, wide in enumerate((gate_w, up_w, down_w)):
        for core in range(NC):
            span = pl.ds(core * each, each)
            targets.append(wide.at[span, :] if i == 2 else wide.at[:, span])
    for copy in copy_in(sources, targets, sems):
        copy.wait()


def stage(own, swapped):
    width, each = own[0].shape
    tall = jax.ShapeDtypeStruct((width, NC * each), BF16)
    wide = jax.ShapeDtypeStruct((NC * each, width), BF16)
    return pl.pallas_call(
        stage_kernel,
        out_shape=[tall, tall, wide],
        in_specs=[ANY] * 6,
        out_specs=[VMEM] * 3,
        scratch_shapes=[pltpu.SemaphoreType.DMA((6,))],
        compiler_params=params(16),
    )(own[0], swapped[0], own[1], swapped[1], own[2], swapped[2])


def experts_kernel(paired, count, forward, backward, *refs):
    refs = list(refs)
    take = lambda n: [refs.pop(0) for _ in range(n)]
    pairs = take(paired)
    rows = [p.at[0] for p in pairs] + take(count - paired if forward else 0)
    grads = [p.at[1] for p in pairs] + take(count - paired if backward else 0)
    pre_in = take(0 if forward else 2)
    gate_w, up_w, down_w = take(3)
    outs = take(count) if forward else []
    ins = take(count) if backward else []
    pre_out = take(0 if backward else 2)
    units, width = down_w.shape
    high = (rows or grads)[0].shape[0]

    def stack(blocks, at):
        if len(blocks) == 1:
            return blocks[0][:, at]
        return stacked(blocks, at)

    gate_pre = up_pre = hidden_grad = jnp.zeros((count * high, units), F32)
    if not forward:
        gate_pre, up_pre = pre_in[0][...], pre_in[1][...]
    for at in strips(width):
        if forward:
            here = stack(rows, at)
            gate_pre += product(here, gate_w[at, :])
            up_pre += product(here, up_w[at, :])
        if backward:
            hidden_grad += product_t(stack(grads, at), down_w[:, at])
    sigma = jax.nn.sigmoid(gate_pre)
    silu = gate_pre * sigma
    if not backward:
        pre_out[0][...] = gate_pre
        pre_out[1][...] = up_pre
    hidden = (silu * up_pre).astype(BF16)
    slope = sigma * (1.0 + gate_pre * (1.0 - sigma))
    gate_grad = (hidden_grad * up_pre * slope).astype(BF16)
    up_grad = (hidden_grad * silu).astype(BF16)
    for at in strips(width):
        if forward:
            got = product(hidden, down_w[:, at])
            for i in range(count):
                outs[i][:, at] = got[i * high : (i + 1) * high].astype(BF16)
        if backward:
            got = product_t(gate_grad, gate_w[at, :]) + product_t(up_grad, up_w[at, :])
            for i in range(count):
                ins[i][:, at] = got[i * high : (i + 1) * high].astype(BF16)


def experts(pairs, rows, grads, weights, pre=()):
    forward, backward = bool(pairs or rows), bool(pairs or grads)
    count = len(pairs) + max(len(rows), len(grads))
    units, width = weights[2].shape
    high = NX * CAP
    shapes = [jax.ShapeDtypeStruct((high, width), BF16)] * (count * (forward + backward))
    if not backward:
        shapes += [jax.ShapeDtypeStruct((count * high, units), F32)] * 2
    given = [*pairs, *rows, *grads, *pre]
    passes = 3 * (forward + backward)
    return pl.pallas_call(
        lambda *refs: experts_kernel(len(pairs), count, forward, backward, *refs),
        out_shape=shapes,
        in_specs=[VMEM] * (len(given) + 3),
        out_specs=[VMEM] * len(shapes),
        compiler_params=params(16),
        cost_estimate=pl.CostEstimate(
            flops=2 * passes * count * high * width * units, bytes_accessed=6 * width * units, transcendentals=0
        ),
    )(*given, *weights)


def on_device(inputs, out_grads, routes, gates, norm_gain, w_gate, w_up, w_down):
    held, incoming = inputs[0], out_grads[0]
    column = (lax.axis_index("expert") // (NZ * NC)).astype(jnp.int32).reshape(1)
    own = (w_gate[0], w_up[0], w_down[0])
    swapped = [move(w, dc=1) for w in own]
    blocks = pick_rows(column, routes[0].T, gates[0].T, held, incoming)
    blocks, swapped[0] = after((blocks, swapped[0]))
    arrived = [blocks[0]] + [move(blocks[k], dx=k) for k in range(1, NX)]
    arrived, weights = after((arrived, stage(own, swapped)))
    first, raw, facts = unfold(arrived, norm_gain)

    sent = after((held, incoming), *blocks)
    passed = (move(sent[0], dy=1), move(sent[1], dy=-1))
    pairs = {0: first, 1: move(first, dz=1), 7: move(first, dz=-1)}
    out_part, in_part = {}, {}

    def work(group):
        got = experts([pairs[j] for j in group], [], [], weights)
        for i, j in enumerate(group):
            out_part[j], in_part[j] = got[i], got[len(group) + i]

    for step in range(3):
        if step > 0:
            pairs[step + 1] = move(pairs[step], dz=1)
            pairs[NZ - step - 1] = move(pairs[NZ - step], dz=-1)
        if step == 2:
            work((0, 1, 7, 2, 6))
        new = (pairs[step + 1], pairs[NZ - step - 1])
        if step == PASSED_BY:
            new, passed = after((new, passed))
        pairs[step + 1], pairs[NZ - step - 1] = after(new, out_part)

    last_rows, last_grads = move(pairs[3][0], dz=1), move(pairs[5][1], dz=-1)
    work((3, 5))
    out_up = move(out_part[5], dz=1)
    in_down = move(in_part[3], dz=-1)
    last_rows = after(last_rows, out_part[3])
    out_part[4], *pre = experts([], [last_rows], [], weights)
    out_down = move(out_part[4], dz=-1)
    last_grads = after(last_grads, out_part[4])
    (in_part[4],) = experts([], [], [last_grads], weights, pre)
    in_up = move(in_part[4], dz=1)

    for step in range(2):
        out_up, in_down = after((out_up, in_down), in_part[4])
        out_up, in_down = add(out_part[6 + step], out_up), add(in_part[2 - step], in_down)
        out_down, in_up = after((out_down, in_up), out_up, in_down)
        out_up, in_down = move(out_up, dz=1), move(in_down, dz=-1)
        out_down, in_up = add(out_part[3 - step], out_down), add(in_part[5 + step], in_up)
        out_down, in_up = move(out_down, dz=-1), move(in_up, dz=1)
    out_down, in_up = add(out_part[1], out_down), add(in_part[7], in_up)
    out_down, in_up = move(out_down, dz=-1), move(in_up, dz=1)

    blocks = finish(finish_out_kernel, out_part[0], out_up, out_down, facts)
    out_blocks = [move(blocks[k], dx=-k, dy=1) for k in FARTHEST]
    blocks = finish(finish_in_kernel, in_part[0], in_up, in_down, facts, raw, norm_gain)
    in_blocks = [move(blocks[k], dx=-k, dy=-1) for k in FARTHEST]
    next_inputs = merge([passed[0]], out_blocks)
    prior_grads = merge([passed[1]], in_blocks)
    return (next_inputs[None], prior_grads[None])


def solution(mesh):
    return jax.shard_map(
        on_device,
        mesh=mesh,
        in_specs=(
            P("pipe", "expert", None),
            P("pipe", "expert", None),
            P("pipe", "expert", None),
            P("pipe", "expert", None),
            P("pipe", None),
            P("pipe", None, "expert"),
            P("pipe", None, "expert"),
            P("pipe", "expert", None),
        ),
        out_specs=(P("pipe", "expert", None), P("pipe", "expert", None)),
        check_vma=False,
    )
```

```python
import jax
import jax.numpy as jnp
from jax import lax
from jax.experimental import pallas as pl
from jax.experimental.pallas import tpu as pltpu
from jax.sharding import PartitionSpec as P

EXP_WIN = 4
CAP = 6
EPSILON = 1e-06
NX, NZ, NC = 4, 8, 2
BOTH = ("pipe", "expert")
STRIPS = 7
FOLDS = 4
PICK_MIB = 52
FARTHEST = (2, 3, 1, 0)
PASSED_BY = 2
ROWS = NX * FOLDS * CAP
NOTE = 128
F32, BF16 = jnp.float32, jnp.bfloat16
VMEM = pl.BlockSpec(memory_space=pltpu.VMEM)
ANY = pl.BlockSpec(memory_space=pl.ANY)


def move(block, dy=0, dx=0, dz=0, dc=0):
    ny = lax.axis_size("pipe")
    route = []
    for y in range(ny):
        for x in range(NX):
            for z in range(NZ):
                for c in range(NC):
                    a = ((y * NX + x) * NZ + z) * NC + c
                    b = (((y + dy) % ny * NX + (x + dx) % NX) * NZ + (z + dz) % NZ) * NC + (c + dc) % NC
                    route.append((a, b))
    return lax.ppermute(block, BOTH, route)


def after(values, *needed):
    return lax.optimization_barrier((values, needed))[0]


def add(part, got):
    return (got.astype(F32) + part.astype(F32)).astype(BF16)


def product(a, b):
    return jnp.dot(a, b, preferred_element_type=F32)


def params(mib):
    return pltpu.CompilerParams(vmem_limit_bytes=mib * 2**20)


def three(value):
    high = value.astype(BF16).astype(F32)
    middle = (value - high).astype(BF16).astype(F32)
    return high, middle, value - high - middle


def strips(width):
    strip = width // STRIPS
    return [slice(s * strip, (s + 1) * strip) for s in range(STRIPS)]


def copy_in(sources, targets, sems):
    copies = [pltpu.make_async_copy(a, b, sems.at[i]) for i, (a, b) in enumerate(zip(sources, targets))]
    for copy in copies:
        copy.start()
    return copies


def folds(width):
    fold = width // FOLDS
    strip = fold // 2
    for s in range(2):
        here = slice(s * strip, (s + 1) * strip)
        yield here, [slice(q * fold + here.start, q * fold + here.stop) for q in range(FOLDS)]


def row_parts(shape, dim):
    row = lax.broadcasted_iota(jnp.int32, shape, dim)
    block = row // (FOLDS * CAP)
    rest = row - block * (FOLDS * CAP)
    fold = rest // CAP
    return block, fold, rest - fold * CAP


def folding(q, dim):
    shape = (ROWS, NX * CAP) if dim == 0 else (NX * CAP, ROWS)
    block, fold, slot = row_parts(shape, dim)
    short = lax.broadcasted_iota(jnp.int32, shape, 1 - dim)
    hit = short == block * CAP + slot
    if q is not None:
        hit = hit & (fold == q)
    return hit.astype(F32).astype(BF16)


def pick_kernel(column, *refs):
    blocks = refs[4 : 4 + NX]
    routes, gates, held, incoming, sems = refs[4 + NX :]
    tokens, width = held.shape
    ids_in, gates_in, *loads_in = copy_in(refs[:4], (routes, gates, held, incoming), sems)
    before = lax.broadcasted_iota(jnp.int32, (tokens, tokens), 0)
    later = lax.broadcasted_iota(jnp.int32, (tokens, tokens), 1)
    order = (before < later).astype(F32).astype(BF16)
    high = FOLDS * CAP
    shape = (high, tokens)
    slot = row_parts(shape, 0)[2].astype(F32)
    token = lax.broadcasted_iota(jnp.int32, shape, 1).astype(F32) + 1.0
    lane = lax.broadcasted_iota(jnp.int32, (high, NOTE), 1)
    picks, loads = [], []
    ids_in.wait()
    gates_in.wait()
    for k in range(NX):
        named = routes[...] == lax.rem(column[0] + k, EXP_WIN)
        mark = jnp.max(named.astype(F32), axis=0, keepdims=True)
        weight = jnp.sum(jnp.where(named, gates[...], 0.0), axis=0, keepdims=True)
        mark = jnp.broadcast_to(mark, shape)
        place = product(mark.astype(BF16), order)
        pick = jnp.where((place == slot) & (mark > 0.0), 1.0, 0.0)
        load = jnp.sum(pick * weight, axis=1, keepdims=True)
        which = jnp.sum(pick * token, axis=1, keepdims=True)
        note = jnp.where(lane == 0, which, 0.0)
        for i, piece in enumerate(three(load)):
            note = jnp.where(lane == i + 1, piece, note)
        blocks[k][:, 2 * width // FOLDS :] = note.astype(BF16)
        picks.append(pick)
        loads.append(load)
    pick = jnp.concatenate(picks, axis=0)
    load = jnp.concatenate(loads, axis=0)
    fold = row_parts((ROWS, tokens), 0)[1]
    parts = [jnp.where(fold == q, pick, 0.0).astype(BF16) for q in range(FOLDS)]
    for i, source in enumerate((held, incoming)):
        loads_in[i].wait()
        for here, plain in folds(width):
            got = sum(product(parts[q], source[:, plain[q]]) for q in range(FOLDS))
            got = (load * got if i else got).astype(BF16)
            for k in range(NX):
                at = slice(i * width // FOLDS + here.start, i * width // FOLDS + here.stop)
                blocks[k][:, at] = got[k * high : (k + 1) * high]


def pick_rows(column, routes, gates, held, incoming):
    tokens, width = held.shape
    high, fold = FOLDS * CAP, width // FOLDS
    return pl.pallas_call(
        pick_kernel,
        out_shape=[jax.ShapeDtypeStruct((high, 2 * fold + NOTE), BF16)] * NX,
        in_specs=[pl.BlockSpec(memory_space=pltpu.SMEM)] + [ANY] * 4,
        out_specs=[VMEM] * NX,
        scratch_shapes=[
            pltpu.VMEM(routes.shape, routes.dtype),
            pltpu.VMEM(gates.shape, gates.dtype),
            pltpu.VMEM((tokens, width), BF16),
            pltpu.VMEM((tokens, width), BF16),
            pltpu.SemaphoreType.DMA((4,)),
        ],
        compiler_params=params(PICK_MIB),
    )(column, routes, gates, held, incoming)


def stacked(blocks, at):
    return jnp.concatenate([b[:, at].astype(F32) for b in blocks], axis=0).astype(BF16)


def unfold_kernel(*refs):
    blocks, gain = refs[:NX], refs[NX]
    pair, raw, facts = refs[NX + 1 :]
    width = gain.shape[1]
    total = jnp.zeros((NX * CAP, 1), F32)
    turns = [folding(q, 1) for q in range(FOLDS)]
    for here, plain in folds(width):
        tall = stacked(blocks, here)
        for q in range(FOLDS):
            part = product(turns[q], tall)
            raw[:, plain[q]] = part.astype(BF16)
            total += jnp.sum(part * part, axis=1, keepdims=True)
    scale = lax.rsqrt(total / width + EPSILON)
    for at in strips(width):
        pair[0, :, at] = (raw[:, at].astype(F32) * scale * gain[:, at]).astype(BF16)
    for here, plain in folds(width):
        tall = stacked(blocks, slice(width // FOLDS + here.start, width // FOLDS + here.stop))
        for q in range(FOLDS):
            pair[1, :, plain[q]] = product(turns[q], tall).astype(BF16)
    note = product(turns[0], stacked(blocks, slice(2 * width // FOLDS, 2 * width // FOLDS + NOTE)))
    load = note[:, 1:2] + note[:, 2:3] + note[:, 3:4]
    lane = lax.broadcasted_iota(jnp.int32, note.shape, 1)
    facts[...] = jnp.where(lane == 0, note, jnp.where(lane == 1, load, scale))


def unfold(blocks, gain):
    width = gain.shape[1]
    chunk = jax.ShapeDtypeStruct((NX * CAP, width), BF16)
    facts = jax.ShapeDtypeStruct((NX * CAP, NOTE), F32)
    return pl.pallas_call(
        unfold_kernel,
        out_shape=[jax.ShapeDtypeStruct((2, *chunk.shape), BF16), chunk, facts],
        in_specs=[VMEM] * (NX + 1),
        out_specs=[VMEM] * 3,
        compiler_params=params(8),
    )(*blocks, gain)


def fold_out(blocks, facts, width, value):
    high = FOLDS * CAP
    turns = [folding(q, 0) for q in range(FOLDS)]
    for here, plain in folds(width):
        tall = sum(product(turns[q], value(plain[q]).astype(BF16)) for q in range(FOLDS)).astype(BF16)
        for k in range(NX):
            blocks[k][:, here] = tall[k * high : (k + 1) * high]
    tall = product(folding(None, 0), facts[...].astype(BF16)).astype(BF16)
    for k in range(NX):
        blocks[k][:, width // FOLDS :] = tall[k * high : (k + 1) * high]


def finish_out_kernel(part, above, below, facts, *blocks):
    def value(at):
        total = part[:, at].astype(F32) + above[:, at].astype(F32) + below[:, at].astype(F32)
        return facts[:, 1:2] * total

    fold_out(blocks, facts, part.shape[1], value)


def finish_in_kernel(part, above, below, facts, raw, gain, *refs):
    blocks, held = refs[:-1], refs[-1]
    width = part.shape[1]
    scale = facts[:, 2:3]
    through = jnp.zeros_like(scale)
    for at in strips(width):
        total = part[:, at].astype(F32) + above[:, at].astype(F32) + below[:, at].astype(F32)
        total = gain[:, at] * total
        held[:, at] = total
        through += jnp.sum(raw[:, at].astype(F32) * total, axis=1, keepdims=True)
    factor = scale * scale * scale / width * through
    fold_out(blocks, facts, width, lambda at: scale * held[:, at] - raw[:, at].astype(F32) * factor)


def finish(kernel, *given):
    high, width = given[0].shape
    scratch = [pltpu.VMEM((high, width), F32)] if kernel is finish_in_kernel else []
    return pl.pallas_call(
        kernel,
        out_shape=[jax.ShapeDtypeStruct((FOLDS * CAP, width // FOLDS + NOTE), BF16)] * NX,
        in_specs=[VMEM] * len(given),
        out_specs=[VMEM] * NX,
        scratch_shapes=scratch,
        compiler_params=params(8),
    )(*given)


def merge_kernel(count, *refs):
    bases, blocks, out_hbm = refs[:count], refs[count : count + NX], refs[count + NX]
    base, out, in_sems, out_sems = refs[count + NX + 1 :]
    tokens, width = base.shape
    fold = width // FOLDS
    spans = [pl.ds(q * fold, fold) for q in range(FOLDS)]
    sources, targets = [], []
    for at in spans:
        top = 0
        for part in bases:
            high = part.shape[0]
            sources.append(part.at[:, at])
            targets.append(base.at[pl.ds(top, high), at])
            top += high
    loads = copy_in(sources, targets, in_sems)
    which = jnp.concatenate([b[:, fold:].astype(F32)[:, 0:1] for b in blocks], axis=0)
    token = lax.broadcasted_iota(jnp.int32, (ROWS, tokens), 1).astype(F32) + 1.0
    part = row_parts((ROWS, tokens), 0)[1]
    stores = []
    for q in range(FOLDS):
        pick = jnp.where((which == token) & (part == q), 1.0, 0.0).T.astype(BF16)
        for copy in loads[q * count : (q + 1) * count]:
            copy.wait()
        for half in range(2):
            here = slice(half * fold // 2, (half + 1) * fold // 2)
            at = slice(q * fold + here.start, q * fold + here.stop)
            more = product(pick, stacked(blocks, here))
            out[:, at] = (base[:, at].astype(F32) + more).astype(BF16)
        copy = pltpu.make_async_copy(out.at[:, spans[q]], out_hbm.at[:, spans[q]], out_sems.at[q])
        copy.start()
        stores.append(copy)
    for copy in stores:
        copy.wait()


def merge(bases, blocks):
    tokens, width = sum(b.shape[0] for b in bases), bases[0].shape[1]
    count = len(bases)
    return pl.pallas_call(
        lambda *refs: merge_kernel(count, *refs),
        out_shape=jax.ShapeDtypeStruct((tokens, width), BF16),
        in_specs=[ANY] * count + [VMEM] * NX,
        out_specs=ANY,
        scratch_shapes=[pltpu.VMEM((tokens, width), BF16)] * 2
        + [pltpu.SemaphoreType.DMA((FOLDS * count,)), pltpu.SemaphoreType.DMA((FOLDS,))],
        compiler_params=params(8),
    )(*bases, *blocks)


def stage_kernel(*refs):
    sources, (gate_w, up_w, down_w, gate_t, up_t, down_t, sems) = refs[:6], refs[6:]
    each = sources[4].shape[0]
    targets = []
    for i, wide in enumerate((gate_w, up_w, down_w)):
        for core in range(NC):
            span = pl.ds(core * each, each)
            targets.append(wide.at[span, :] if i == 2 else wide.at[:, span])
    copies = copy_in(sources, targets, sems)
    width = down_w.shape[1]
    for i, (wide, turned) in enumerate(((gate_w, gate_t), (up_w, up_t), (down_w, down_t))):
        for copy in copies[NC * i : NC * (i + 1)]:
            copy.wait()
        for at in strips(width):
            if i == 2:
                turned[at, :] = wide[:, at].T
            else:
                turned[:, at] = wide[at, :].T


def stage(own, swapped):
    width, each = own[0].shape
    tall = jax.ShapeDtypeStruct((width, NC * each), BF16)
    wide = jax.ShapeDtypeStruct((NC * each, width), BF16)
    return pl.pallas_call(
        stage_kernel,
        out_shape=[tall, tall, wide, wide, wide, tall],
        in_specs=[ANY] * 6,
        out_specs=[VMEM] * 6,
        scratch_shapes=[pltpu.SemaphoreType.DMA((6,))],
        compiler_params=params(16),
    )(own[0], swapped[0], own[1], swapped[1], own[2], swapped[2])


def experts_kernel(paired, count, forward, backward, *refs):
    refs = list(refs)
    take = lambda n: [refs.pop(0) for _ in range(n)]
    pairs = take(paired)
    rows = [p.at[0] for p in pairs] + take(count - paired if forward else 0)
    grads = [p.at[1] for p in pairs] + take(count - paired if backward else 0)
    pre_in = take(0 if forward else 2)
    gate_w, up_w, down_w = take(3) if forward else (None, None, None)
    gate_t, up_t, down_t = take(3) if backward else (None, None, None)
    outs = take(count) if forward else []
    ins = take(count) if backward else []
    pre_out = take(0 if backward else 2)
    units, width = down_w.shape if forward else gate_t.shape
    high = (rows or grads)[0].shape[0]

    def stack(blocks, at):
        if len(blocks) == 1:
            return blocks[0][:, at]
        return stacked(blocks, at)

    gate_pre = up_pre = hidden_grad = jnp.zeros((count * high, units), F32)
    if not forward:
        gate_pre, up_pre = pre_in[0][...], pre_in[1][...]
    for at in strips(width):
        if forward:
            here = stack(rows, at)
            gate_pre += product(here, gate_w[at, :])
            up_pre += product(here, up_w[at, :])
        if backward:
            hidden_grad += product(stack(grads, at), down_t[at, :])
    sigma = jax.nn.sigmoid(gate_pre)
    silu = gate_pre * sigma
    if not backward:
        pre_out[0][...] = gate_pre
        pre_out[1][...] = up_pre
    hidden = (silu * up_pre).astype(BF16)
    slope = sigma * (1.0 + gate_pre * (1.0 - sigma))
    gate_grad = (hidden_grad * up_pre * slope).astype(BF16)
    up_grad = (hidden_grad * silu).astype(BF16)
    for at in strips(width):
        if forward:
            got = product(hidden, down_w[:, at])
            for i in range(count):
                outs[i][:, at] = got[i * high : (i + 1) * high].astype(BF16)
        if backward:
            got = product(gate_grad, gate_t[:, at]) + product(up_grad, up_t[:, at])
            for i in range(count):
                ins[i][:, at] = got[i * high : (i + 1) * high].astype(BF16)


def experts(pairs, rows, grads, weights, pre=()):
    forward, backward = bool(pairs or rows), bool(pairs or grads)
    count = len(pairs) + max(len(rows), len(grads))
    units, width = weights[2].shape
    high = NX * CAP
    shapes = [jax.ShapeDtypeStruct((high, width), BF16)] * (count * (forward + backward))
    if not backward:
        shapes += [jax.ShapeDtypeStruct((count * high, units), F32)] * 2
    given = [*pairs, *rows, *grads, *pre, *weights[0 if forward else 3 : 6 if backward else 3]]
    passes = 3 * (forward + backward)
    return pl.pallas_call(
        lambda *refs: experts_kernel(len(pairs), count, forward, backward, *refs),
        out_shape=shapes,
        in_specs=[VMEM] * len(given),
        out_specs=[VMEM] * len(shapes),
        compiler_params=params(16),
        cost_estimate=pl.CostEstimate(
            flops=2 * passes * count * high * width * units, bytes_accessed=6 * width * units, transcendentals=0
        ),
    )(*given)


def on_device(inputs, out_grads, routes, gates, norm_gain, w_gate, w_up, w_down):
    held, incoming = inputs[0], out_grads[0]
    column = (lax.axis_index("expert") // (NZ * NC)).astype(jnp.int32).reshape(1)
    own = (w_gate[0], w_up[0], w_down[0])
    swapped = [move(w, dc=1) for w in own]
    blocks = pick_rows(column, routes[0].T, gates[0].T, held, incoming)
    blocks, swapped[0] = after((blocks, swapped[0]))
    arrived = [blocks[0]] + [move(blocks[k], dx=k) for k in range(1, NX)]
    arrived, weights = after((arrived, stage(own, swapped)))
    first, raw, facts = unfold(arrived, norm_gain)

    sent = after((held, incoming), *blocks)
    passed = (move(sent[0], dy=1), move(sent[1], dy=-1))
    pairs = {0: first, 1: move(first, dz=1), 7: move(first, dz=-1)}
    out_part, in_part = {}, {}

    def work(group):
        got = experts([pairs[j] for j in group], [], [], weights)
        for i, j in enumerate(group):
            out_part[j], in_part[j] = got[i], got[len(group) + i]

    for step in range(3):
        if step > 0:
            pairs[step + 1] = move(pairs[step], dz=1)
            pairs[NZ - step - 1] = move(pairs[NZ - step], dz=-1)
        if step == 2:
            work((0, 1, 7, 2, 6))
        new = (pairs[step + 1], pairs[NZ - step - 1])
        if step == PASSED_BY:
            new, passed = after((new, passed))
        pairs[step + 1], pairs[NZ - step - 1] = after(new, out_part)

    last_rows, last_grads = move(pairs[3][0], dz=1), move(pairs[5][1], dz=-1)
    work((3, 5))
    out_up = move(out_part[5], dz=1)
    in_down = move(in_part[3], dz=-1)
    last_rows = after(last_rows, out_part[3])
    out_part[4], *pre = experts([], [last_rows], [], weights)
    out_down = move(out_part[4], dz=-1)
    last_grads = after(last_grads, out_part[4])
    (in_part[4],) = experts([], [], [last_grads], weights, pre)
    in_up = move(in_part[4], dz=1)

    for step in range(2):
        out_up, in_down = after((out_up, in_down), in_part[4])
        out_up, in_down = add(out_part[6 + step], out_up), add(in_part[2 - step], in_down)
        out_down, in_up = after((out_down, in_up), out_up, in_down)
        out_up, in_down = move(out_up, dz=1), move(in_down, dz=-1)
        out_down, in_up = add(out_part[3 - step], out_down), add(in_part[5 + step], in_up)
        out_down, in_up = move(out_down, dz=-1), move(in_up, dz=1)
    out_down, in_up = add(out_part[1], out_down), add(in_part[7], in_up)
    out_down, in_up = move(out_down, dz=-1), move(in_up, dz=1)

    blocks = finish(finish_out_kernel, out_part[0], out_up, out_down, facts)
    out_blocks = [move(blocks[k], dx=-k, dy=1) for k in FARTHEST]
    blocks = finish(finish_in_kernel, in_part[0], in_up, in_down, facts, raw, norm_gain)
    in_blocks = [move(blocks[k], dx=-k, dy=-1) for k in FARTHEST]
    next_inputs = merge([passed[0]], out_blocks)
    prior_grads = merge([passed[1]], in_blocks)
    return (next_inputs[None], prior_grads[None])


def solution(mesh):
    return jax.shard_map(
        on_device,
        mesh=mesh,
        in_specs=(
            P("pipe", "expert", None),
            P("pipe", "expert", None),
            P("pipe", "expert", None),
            P("pipe", "expert", None),
            P("pipe", None),
            P("pipe", None, "expert"),
            P("pipe", None, "expert"),
            P("pipe", "expert", None),
        ),
        out_specs=(P("pipe", "expert", None), P("pipe", "expert", None)),
        check_vma=False,
    )
```

```python
import jax
import jax.numpy as jnp
from jax import lax
from jax.experimental import pallas as pl
from jax.experimental.pallas import tpu as pltpu
from jax.sharding import PartitionSpec as P

EXP_WIN = 4
CAP = 6
EPSILON = 1e-06
NX, NZ, NC = 4, 8, 2
BOTH = ("pipe", "expert")
STRIPS = 7
FOLDS = 4
PICK_MIB = 52
FARTHEST = (2, 3, 1, 0)
PASSED_BY = 2
ROWS = NX * FOLDS * CAP
NOTE = 128
F32, BF16 = jnp.float32, jnp.bfloat16
VMEM = pl.BlockSpec(memory_space=pltpu.VMEM)
ANY = pl.BlockSpec(memory_space=pl.ANY)


def move(block, dy=0, dx=0, dz=0, dc=0):
    ny = lax.axis_size("pipe")
    route = []
    for y in range(ny):
        for x in range(NX):
            for z in range(NZ):
                for c in range(NC):
                    a = ((y * NX + x) * NZ + z) * NC + c
                    b = (((y + dy) % ny * NX + (x + dx) % NX) * NZ + (z + dz) % NZ) * NC + (c + dc) % NC
                    route.append((a, b))
    return lax.ppermute(block, BOTH, route)


def after(values, *needed):
    return lax.optimization_barrier((values, needed))[0]


def add(part, got):
    return (got.astype(F32) + part.astype(F32)).astype(BF16)


def product(a, b):
    return jnp.dot(a, b, preferred_element_type=F32)


def params(mib):
    return pltpu.CompilerParams(vmem_limit_bytes=mib * 2**20)


def three(value):
    high = value.astype(BF16).astype(F32)
    middle = (value - high).astype(BF16).astype(F32)
    return high, middle, value - high - middle


def strips(width):
    strip = width // STRIPS
    return [slice(s * strip, (s + 1) * strip) for s in range(STRIPS)]


def copy_in(sources, targets, sems):
    copies = [pltpu.make_async_copy(a, b, sems.at[i]) for i, (a, b) in enumerate(zip(sources, targets))]
    for copy in copies:
        copy.start()
    return copies


def folds(width):
    fold = width // FOLDS
    strip = fold // 2
    for s in range(2):
        here = slice(s * strip, (s + 1) * strip)
        yield here, [slice(q * fold + here.start, q * fold + here.stop) for q in range(FOLDS)]


def row_parts(shape, dim):
    row = lax.broadcasted_iota(jnp.int32, shape, dim)
    block = row // (FOLDS * CAP)
    rest = row - block * (FOLDS * CAP)
    fold = rest // CAP
    return block, fold, rest - fold * CAP


def folding(q, dim):
    shape = (ROWS, NX * CAP) if dim == 0 else (NX * CAP, ROWS)
    block, fold, slot = row_parts(shape, dim)
    short = lax.broadcasted_iota(jnp.int32, shape, 1 - dim)
    hit = short == block * CAP + slot
    if q is not None:
        hit = hit & (fold == q)
    return hit.astype(F32).astype(BF16)


def pick_kernel(column, *refs):
    blocks = refs[4 : 4 + NX]
    routes, gates, held, incoming, sems = refs[4 + NX :]
    tokens, width = held.shape
    ids_in, gates_in, *loads_in = copy_in(refs[:4], (routes, gates, held, incoming), sems)
    before = lax.broadcasted_iota(jnp.int32, (tokens, tokens), 0)
    later = lax.broadcasted_iota(jnp.int32, (tokens, tokens), 1)
    order = (before < later).astype(F32).astype(BF16)
    high = FOLDS * CAP
    shape = (high, tokens)
    slot = row_parts(shape, 0)[2].astype(F32)
    token = lax.broadcasted_iota(jnp.int32, shape, 1).astype(F32) + 1.0
    lane = lax.broadcasted_iota(jnp.int32, (high, NOTE), 1)
    picks, loads = [], []
    ids_in.wait()
    gates_in.wait()
    for k in range(NX):
        named = routes[...] == lax.rem(column[0] + k, EXP_WIN)
        mark = jnp.max(named.astype(F32), axis=0, keepdims=True)
        weight = jnp.sum(jnp.where(named, gates[...], 0.0), axis=0, keepdims=True)
        mark = jnp.broadcast_to(mark, shape)
        place = product(mark.astype(BF16), order)
        pick = jnp.where((place == slot) & (mark > 0.0), 1.0, 0.0)
        load = jnp.sum(pick * weight, axis=1, keepdims=True)
        which = jnp.sum(pick * token, axis=1, keepdims=True)
        note = jnp.where(lane == 0, which, 0.0)
        for i, piece in enumerate(three(load)):
            note = jnp.where(lane == i + 1, piece, note)
        blocks[k][:, 2 * width // FOLDS :] = note.astype(BF16)
        picks.append(pick)
        loads.append(load)
    pick = jnp.concatenate(picks, axis=0)
    load = jnp.concatenate(loads, axis=0)
    fold = row_parts((ROWS, tokens), 0)[1]
    parts = [jnp.where(fold == q, pick, 0.0).astype(BF16) for q in range(FOLDS)]
    for i, source in enumerate((held, incoming)):
        loads_in[i].wait()
        for here, plain in folds(width):
            got = sum(product(parts[q], source[:, plain[q]]) for q in range(FOLDS))
            got = (load * got if i else got).astype(BF16)
            for k in range(NX):
                at = slice(i * width // FOLDS + here.start, i * width // FOLDS + here.stop)
                blocks[k][:, at] = got[k * high : (k + 1) * high]


def pick_rows(column, routes, gates, held, incoming):
    tokens, width = held.shape
    high, fold = FOLDS * CAP, width // FOLDS
    return pl.pallas_call(
        pick_kernel,
        out_shape=[jax.ShapeDtypeStruct((high, 2 * fold + NOTE), BF16)] * NX,
        in_specs=[pl.BlockSpec(memory_space=pltpu.SMEM)] + [ANY] * 4,
        out_specs=[VMEM] * NX,
        scratch_shapes=[
            pltpu.VMEM(routes.shape, routes.dtype),
            pltpu.VMEM(gates.shape, gates.dtype),
            pltpu.VMEM((tokens, width), BF16),
            pltpu.VMEM((tokens, width), BF16),
            pltpu.SemaphoreType.DMA((4,)),
        ],
        compiler_params=params(PICK_MIB),
    )(column, routes, gates, held, incoming)


def stacked(blocks, at):
    return jnp.concatenate([b[:, at].astype(F32) for b in blocks], axis=0).astype(BF16)


def unfold_kernel(*refs):
    blocks, gain = refs[:NX], refs[NX]
    pair, raw, facts = refs[NX + 1 :]
    width = gain.shape[1]
    total = jnp.zeros((NX * CAP, 1), F32)
    turns = [folding(q, 1) for q in range(FOLDS)]
    for here, plain in folds(width):
        tall = stacked(blocks, here)
        for q in range(FOLDS):
            part = product(turns[q], tall)
            raw[:, plain[q]] = part.astype(BF16)
            total += jnp.sum(part * part, axis=1, keepdims=True)
    scale = lax.rsqrt(total / width + EPSILON)
    for at in strips(width):
        pair[0, :, at] = (raw[:, at].astype(F32) * scale * gain[:, at]).astype(BF16)
    for here, plain in folds(width):
        tall = stacked(blocks, slice(width // FOLDS + here.start, width // FOLDS + here.stop))
        for q in range(FOLDS):
            pair[1, :, plain[q]] = product(turns[q], tall).astype(BF16)
    note = product(turns[0], stacked(blocks, slice(2 * width // FOLDS, 2 * width // FOLDS + NOTE)))
    load = note[:, 1:2] + note[:, 2:3] + note[:, 3:4]
    lane = lax.broadcasted_iota(jnp.int32, note.shape, 1)
    facts[...] = jnp.where(lane == 0, note, jnp.where(lane == 1, load, scale))


def unfold(blocks, gain):
    width = gain.shape[1]
    chunk = jax.ShapeDtypeStruct((NX * CAP, width), BF16)
    facts = jax.ShapeDtypeStruct((NX * CAP, NOTE), F32)
    return pl.pallas_call(
        unfold_kernel,
        out_shape=[jax.ShapeDtypeStruct((2, *chunk.shape), BF16), chunk, facts],
        in_specs=[VMEM] * (NX + 1),
        out_specs=[VMEM] * 3,
        compiler_params=params(8),
    )(*blocks, gain)


def fold_out(blocks, facts, width, value):
    high = FOLDS * CAP
    turns = [folding(q, 0) for q in range(FOLDS)]
    for here, plain in folds(width):
        tall = sum(product(turns[q], value(plain[q]).astype(BF16)) for q in range(FOLDS)).astype(BF16)
        for k in range(NX):
            blocks[k][:, here] = tall[k * high : (k + 1) * high]
    tall = product(folding(None, 0), facts[...].astype(BF16)).astype(BF16)
    for k in range(NX):
        blocks[k][:, width // FOLDS :] = tall[k * high : (k + 1) * high]


def finish_out_kernel(part, above, below, facts, *blocks):
    def value(at):
        total = part[:, at].astype(F32) + above[:, at].astype(F32) + below[:, at].astype(F32)
        return facts[:, 1:2] * total

    fold_out(blocks, facts, part.shape[1], value)


def finish_in_kernel(part, above, below, facts, raw, gain, *refs):
    blocks, held = refs[:-1], refs[-1]
    width = part.shape[1]
    scale = facts[:, 2:3]
    through = jnp.zeros_like(scale)
    for at in strips(width):
        total = part[:, at].astype(F32) + above[:, at].astype(F32) + below[:, at].astype(F32)
        total = gain[:, at] * total
        held[:, at] = total
        through += jnp.sum(raw[:, at].astype(F32) * total, axis=1, keepdims=True)
    factor = scale * scale * scale / width * through
    fold_out(blocks, facts, width, lambda at: scale * held[:, at] - raw[:, at].astype(F32) * factor)


def finish(kernel, *given):
    high, width = given[0].shape
    scratch = [pltpu.VMEM((high, width), F32)] if kernel is finish_in_kernel else []
    return pl.pallas_call(
        kernel,
        out_shape=[jax.ShapeDtypeStruct((FOLDS * CAP, width // FOLDS + NOTE), BF16)] * NX,
        in_specs=[VMEM] * len(given),
        out_specs=[VMEM] * NX,
        scratch_shapes=scratch,
        compiler_params=params(8),
    )(*given)


def merge_kernel(count, *refs):
    bases, blocks, out_hbm = refs[:count], refs[count : count + NX], refs[count + NX]
    base, out, in_sems, out_sems = refs[count + NX + 1 :]
    tokens, width = base.shape
    fold = width // FOLDS
    spans = [pl.ds(q * fold, fold) for q in range(FOLDS)]
    sources, targets = [], []
    for at in spans:
        top = 0
        for part in bases:
            high = part.shape[0]
            sources.append(part.at[:, at])
            targets.append(base.at[pl.ds(top, high), at])
            top += high
    loads = copy_in(sources, targets, in_sems)
    which = jnp.concatenate([b[:, fold:].astype(F32)[:, 0:1] for b in blocks], axis=0)
    token = lax.broadcasted_iota(jnp.int32, (ROWS, tokens), 1).astype(F32) + 1.0
    part = row_parts((ROWS, tokens), 0)[1]
    stores = []
    for q in range(FOLDS):
        pick = jnp.where((which == token) & (part == q), 1.0, 0.0).T.astype(BF16)
        for copy in loads[q * count : (q + 1) * count]:
            copy.wait()
        for half in range(2):
            here = slice(half * fold // 2, (half + 1) * fold // 2)
            at = slice(q * fold + here.start, q * fold + here.stop)
            more = product(pick, stacked(blocks, here))
            out[:, at] = (base[:, at].astype(F32) + more).astype(BF16)
        copy = pltpu.make_async_copy(out.at[:, spans[q]], out_hbm.at[:, spans[q]], out_sems.at[q])
        copy.start()
        stores.append(copy)
    for copy in stores:
        copy.wait()


def merge(bases, blocks):
    tokens, width = sum(b.shape[0] for b in bases), bases[0].shape[1]
    count = len(bases)
    return pl.pallas_call(
        lambda *refs: merge_kernel(count, *refs),
        out_shape=jax.ShapeDtypeStruct((tokens, width), BF16),
        in_specs=[ANY] * count + [VMEM] * NX,
        out_specs=ANY,
        scratch_shapes=[pltpu.VMEM((tokens, width), BF16)] * 2
        + [pltpu.SemaphoreType.DMA((FOLDS * count,)), pltpu.SemaphoreType.DMA((FOLDS,))],
        compiler_params=params(8),
    )(*bases, *blocks)


def stage_kernel(*refs):
    sources, (gate_w, up_w, down_w, gate_t, up_t, down_t, sems) = refs[:6], refs[6:]
    each = sources[4].shape[0]
    targets = []
    for i, wide in enumerate((gate_w, up_w, down_w)):
        for core in range(NC):
            span = pl.ds(core * each, each)
            targets.append(wide.at[span, :] if i == 2 else wide.at[:, span])
    copies = copy_in(sources, targets, sems)
    width = down_w.shape[1]
    for i, (wide, turned) in enumerate(((gate_w, gate_t), (up_w, up_t), (down_w, down_t))):
        for copy in copies[NC * i : NC * (i + 1)]:
            copy.wait()
        for at in strips(width):
            if i == 2:
                turned[at, :] = wide[:, at].T
            else:
                turned[:, at] = wide[at, :].T


def stage(own, swapped):
    width, each = own[0].shape
    tall = jax.ShapeDtypeStruct((width, NC * each), BF16)
    wide = jax.ShapeDtypeStruct((NC * each, width), BF16)
    return pl.pallas_call(
        stage_kernel,
        out_shape=[tall, tall, wide, wide, wide, tall],
        in_specs=[ANY] * 6,
        out_specs=[VMEM] * 6,
        scratch_shapes=[pltpu.SemaphoreType.DMA((6,))],
        compiler_params=params(16),
    )(own[0], swapped[0], own[1], swapped[1], own[2], swapped[2])


def experts_kernel(paired, count, forward, backward, *refs):
    refs = list(refs)
    take = lambda n: [refs.pop(0) for _ in range(n)]
    pairs = take(paired)
    rows = [p.at[0] for p in pairs] + take(count - paired if forward else 0)
    grads = [p.at[1] for p in pairs] + take(count - paired if backward else 0)
    pre_in = take(0 if forward else 2)
    gate_w, up_w, down_w = take(3) if forward else (None, None, None)
    gate_t, up_t, down_t = take(3) if backward else (None, None, None)
    outs = take(count) if forward else []
    ins = take(count) if backward else []
    pre_out = take(0 if backward else 2)
    units, width = down_w.shape if forward else gate_t.shape
    high = (rows or grads)[0].shape[0]

    def stack(blocks, at):
        if len(blocks) == 1:
            return blocks[0][:, at]
        return stacked(blocks, at)

    gate_pre = up_pre = hidden_grad = jnp.zeros((count * high, units), F32)
    if not forward:
        gate_pre, up_pre = pre_in[0][...], pre_in[1][...]
    for at in strips(width):
        if forward:
            here = stack(rows, at)
            gate_pre += product(here, gate_w[at, :])
            up_pre += product(here, up_w[at, :])
        if backward:
            hidden_grad += product(stack(grads, at), down_t[at, :])
    sigma = jax.nn.sigmoid(gate_pre)
    silu = gate_pre * sigma
    if not backward:
        pre_out[0][...] = gate_pre
        pre_out[1][...] = up_pre
    hidden = (silu * up_pre).astype(BF16)
    slope = sigma * (1.0 + gate_pre * (1.0 - sigma))
    gate_grad = (hidden_grad * up_pre * slope).astype(BF16)
    up_grad = (hidden_grad * silu).astype(BF16)
    for at in strips(width):
        if forward:
            got = product(hidden, down_w[:, at])
            for i in range(count):
                outs[i][:, at] = got[i * high : (i + 1) * high].astype(BF16)
        if backward:
            got = product(gate_grad, gate_t[:, at]) + product(up_grad, up_t[:, at])
            for i in range(count):
                ins[i][:, at] = got[i * high : (i + 1) * high].astype(BF16)


def experts(pairs, rows, grads, weights, pre=()):
    forward, backward = bool(pairs or rows), bool(pairs or grads)
    count = len(pairs) + max(len(rows), len(grads))
    units, width = weights[2].shape
    high = NX * CAP
    shapes = [jax.ShapeDtypeStruct((high, width), BF16)] * (count * (forward + backward))
    if not backward:
        shapes += [jax.ShapeDtypeStruct((count * high, units), F32)] * 2
    given = [*pairs, *rows, *grads, *pre, *weights[0 if forward else 3 : 6 if backward else 3]]
    passes = 3 * (forward + backward)
    return pl.pallas_call(
        lambda *refs: experts_kernel(len(pairs), count, forward, backward, *refs),
        out_shape=shapes,
        in_specs=[VMEM] * len(given),
        out_specs=[VMEM] * len(shapes),
        compiler_params=params(16),
        cost_estimate=pl.CostEstimate(
            flops=2 * passes * count * high * width * units, bytes_accessed=6 * width * units, transcendentals=0
        ),
    )(*given)


def on_device(inputs, out_grads, routes, gates, norm_gain, w_gate, w_up, w_down):
    held, incoming = inputs[0], out_grads[0]
    column = (lax.axis_index("expert") // (NZ * NC)).astype(jnp.int32).reshape(1)
    own = (w_gate[0], w_up[0], w_down[0])
    swapped = [move(w, dc=1) for w in own]
    blocks = pick_rows(column, routes[0].T, gates[0].T, held, incoming)
    blocks, swapped[0] = after((blocks, swapped[0]))
    far = {k: move(blocks[k], dx=k) for k in FARTHEST[:1] + (1, 3)}
    arrived = [blocks[0]] + [far[k] for k in range(1, NX)]
    arrived, weights = after((arrived, stage(own, swapped)))
    first, raw, facts = unfold(arrived, norm_gain)

    sent = after((held, incoming), *blocks)
    passed = (move(sent[0], dy=1), move(sent[1], dy=-1))
    pairs = {0: first, 1: move(first, dz=1), 7: move(first, dz=-1)}
    out_part, in_part = {}, {}

    def work(group):
        got = experts([pairs[j] for j in group], [], [], weights)
        for i, j in enumerate(group):
            out_part[j], in_part[j] = got[i], got[len(group) + i]

    for step in range(3):
        if step > 0:
            pairs[step + 1] = move(pairs[step], dz=1)
            pairs[NZ - step - 1] = move(pairs[NZ - step], dz=-1)
        if step == 2:
            work((0, 1, 7, 2, 6))
        new = (pairs[step + 1], pairs[NZ - step - 1])
        if step == PASSED_BY:
            new, passed = after((new, passed))
        pairs[step + 1], pairs[NZ - step - 1] = after(new, out_part)

    last_rows, last_grads = move(pairs[3][0], dz=1), move(pairs[5][1], dz=-1)
    work((3, 5))
    out_up = move(out_part[5], dz=1)
    in_down = move(in_part[3], dz=-1)
    last_rows = after(last_rows, out_part[3])
    out_part[4], *pre = experts([], [last_rows], [], weights)
    out_down = move(out_part[4], dz=-1)
    last_grads = after(last_grads, out_part[4])
    (in_part[4],) = experts([], [], [last_grads], weights, pre)
    in_up = move(in_part[4], dz=1)

    for step in range(2):
        out_up, in_down = after((out_up, in_down), in_part[4])
        out_up, in_down = add(out_part[6 + step], out_up), add(in_part[2 - step], in_down)
        out_down, in_up = after((out_down, in_up), out_up, in_down)
        out_up, in_down = move(out_up, dz=1), move(in_down, dz=-1)
        out_down, in_up = add(out_part[3 - step], out_down), add(in_part[5 + step], in_up)
        out_down, in_up = move(out_down, dz=-1), move(in_up, dz=1)
    out_down, in_up = add(out_part[1], out_down), add(in_part[7], in_up)
    out_down, in_up = move(out_down, dz=-1), move(in_up, dz=1)

    blocks = finish(finish_out_kernel, out_part[0], out_up, out_down, facts)
    out_blocks = [move(blocks[k], dx=-k, dy=1) for k in FARTHEST]
    blocks = finish(finish_in_kernel, in_part[0], in_up, in_down, facts, raw, norm_gain)
    in_blocks = [move(blocks[k], dx=-k, dy=-1) for k in FARTHEST]
    next_inputs = merge([passed[0]], out_blocks)
    prior_grads = merge([passed[1]], in_blocks)
    return (next_inputs[None], prior_grads[None])


def solution(mesh):
    return jax.shard_map(
        on_device,
        mesh=mesh,
        in_specs=(
            P("pipe", "expert", None),
            P("pipe", "expert", None),
            P("pipe", "expert", None),
            P("pipe", "expert", None),
            P("pipe", None),
            P("pipe", None, "expert"),
            P("pipe", None, "expert"),
            P("pipe", "expert", None),
        ),
        out_specs=(P("pipe", "expert", None), P("pipe", "expert", None)),
        check_vma=False,
    )
```
